256 devices in a mesh: space: 32 (over z_lo, y, core), fac: 8 (over z_hi, x).
Axes of the slice: x: 4, y: 4, z: 8 (z_hi: 2, z_lo: 4; z = z_hi * 4 + z_lo), core: 2. Of those that a mesh axis runs over, the one named last changes fastest.
Arguments:
- activations: bfloat16 [8, 64, 16, 16, 128], P('fac', 'space'), may hold values from -60 to 60
- out_grad: bfloat16 [8, 64, 16, 16, 128], P('fac', 'space'), may hold values from -60 to 60
- kernel: bfloat16 [27, 128, 128], replicated, may hold values from -0.109375 to 0.109375
Outputs:
- in_grad: bfloat16 [8, 64, 16, 16, 128], P('fac', 'space')
- update: float32 [27, 128, 128], P(None, 'fac')
The draws below stay inside these ranges and needn't reach their ends.
All inputs are finite; a program needn't handle non-finite values.
Results may differ from the reference program's by a relative error of at most 0.0014.
Values may be sent and summed in bfloat16 or wider, within the bound.
No kernel may reach another device: no remote copies, remote signals or barrier semaphores. Data moves between devices by JAX's collectives and lax.ppermute only.
A program may use at most 128 MiB of HBM per device.

```python
import math
import jax
import jax.numpy as jnp
from jax import lax

C = 128
KS = 27
NY = 16
NZ = 16
SLABS = 8
NX = 64
N_FAC = 8


def field_draw(key, shifts, axis_roll):
    shape = (SLABS, NX, NY, NZ, C)
    first, second, third = jax.random.split(key, 3)
    base = jax.random.truncated_normal(first, -4.0, 4.0, shape, jnp.float32)
    mixed = base + 0.7 * jnp.roll(base, shifts, axis=4) + 0.5 * jnp.roll(base, 1, axis=axis_roll)
    channel_scale = jnp.exp(jax.random.uniform(second, (C,), jnp.float32, math.log(0.3), math.log(3.0)))
    cell_scale = jnp.exp(jax.random.uniform(third, (SLABS, NX, NY, NZ, 1), jnp.float32, math.log(0.5), math.log(2.0)))
    return (mixed * channel_scale * cell_scale).astype(jnp.bfloat16)


def draw_activations(key, part):
    key = jax.random.fold_in(key, 11)
    return field_draw(key, 1, 3)


def draw_out_grad(key, part):
    key = jax.random.fold_in(key, 12)
    return field_draw(key, 3, 2)


def bell_draw(key, dims, scale, most, held_as=jnp.bfloat16):
    values = jax.random.normal(key, dims, jnp.float32) * scale
    return jnp.minimum(jnp.maximum(values, -most), most).astype(held_as)


def setup_inputs(seed: int = 0) -> dict:
    keys = jax.random.split(jax.random.key(seed), 4)
    return {
        "activations": draw_activations(jax.random.fold_in(keys[3], 71), 0),
        "out_grad": draw_out_grad(jax.random.fold_in(keys[3], 71), 0),
        "kernel": bell_draw(keys[2], (KS, C, C), (KS * C) ** -0.5, 0.109375),
    }


damping = 0.1
clip_rate = 0.05

def offsets():
    return [(a, b, c) for a in (-1, 0, 1) for b in (-1, 0, 1) for c in (-1, 0, 1)]

def window(padded, shift, extent):
    return padded[1 + shift[0]:1 + shift[0] + extent[0], 1 + shift[1]:1 + shift[1] + extent[1], 1 + shift[2]:1 + shift[2] + extent[2]]

def slab_terms(padded_in, padded_cot, kernel, groups, extent):
    channels = padded_in.shape[-1]
    width = channels // groups
    cells = extent[0] * extent[1] * extent[2]
    rows_cot = window(padded_cot, (0, 0, 0), extent).reshape(cells, channels)
    gram_list = []
    grad_list = []
    for block_index in range(groups):
        lower = block_index * width
        pieces = [window(padded_in, shift, extent)[..., lower:lower + width].reshape(cells, width) for shift in offsets()]
        patch = jnp.concatenate(pieces, axis=1)
        gram_list.append(jnp.dot(patch.T.astype(jnp.float32), patch.astype(jnp.float32), preferred_element_type=jnp.float32))
        grad_list.append(jnp.dot(patch.T.astype(jnp.float32), rows_cot.astype(jnp.float32), preferred_element_type=jnp.float32))
    cot_gram = jnp.dot(rows_cot.T.astype(jnp.float32), rows_cot.astype(jnp.float32), preferred_element_type=jnp.float32)
    in_grad = jnp.zeros((cells, channels), jnp.float32)
    for tap_index, shift in enumerate(offsets()):
        back = (-shift[0], -shift[1], -shift[2])
        rows = window(padded_cot, back, extent).reshape(cells, channels)
        in_grad = in_grad + jnp.dot(rows.astype(jnp.float32), kernel[tap_index].T.astype(jnp.float32), preferred_element_type=jnp.float32)
    return (jnp.stack(gram_list), jnp.stack(grad_list), cot_gram, in_grad.astype(jnp.bfloat16))

def solve_block(gram_sum, grad_sum, right_chol, count):
    order = gram_sum.shape[0]
    left_mat = gram_sum / count + damping * jnp.eye(order, dtype=jnp.float32)
    left_chol = jnp.linalg.cholesky(left_mat)
    scaled = grad_sum / math.sqrt(count)
    half = jax.scipy.linalg.cho_solve((left_chol, True), scaled)
    raw = jax.scipy.linalg.cho_solve((right_chol, True), half.T).T
    return (raw, scaled)

def reference(activations, out_grad, kernel):
    slabs, size_x, size_y, size_z, channels = activations.shape
    extent = (size_x, size_y, size_z)
    width = channels // N_FAC
    order = 27 * width
    pads = ((1, 1), (1, 1), (1, 1), (0, 0))

    def one_slab(carry, pair):
        inputs, cotangent = pair
        grams, grads, cot_gram, in_grad = slab_terms(jnp.pad(inputs, pads), jnp.pad(cotangent, pads), kernel, N_FAC, extent)
        return ((carry[0] + grams, carry[1] + grads, carry[2] + cot_gram), in_grad.reshape(inputs.shape))
    start = (jnp.zeros((N_FAC, order, order), jnp.float32), jnp.zeros((N_FAC, order, channels), jnp.float32), jnp.zeros((channels, channels), jnp.float32))
    (grams, grads, cot_gram), in_grad = lax.scan(one_slab, start, (activations, out_grad))
    count = float(slabs * size_x * size_y * size_z)
    right_mat = cot_gram / count + damping * jnp.eye(channels, dtype=jnp.float32)
    right_chol = jnp.linalg.cholesky(right_mat)
    raw_list = []
    total = jnp.float32(0.0)
    for block_index in range(N_FAC):
        raw, scaled = solve_block(grams[block_index], grads[block_index], right_chol, count)
        raw_list.append(raw)
        total = total + jnp.sum(raw * scaled)
    factor = jnp.sqrt(clip_rate * kernel.size / total)
    stacked = jnp.stack(raw_list).reshape(N_FAC, 27, width, channels)
    update = jnp.transpose(stacked, (1, 0, 2, 3)).reshape(27, channels, channels) * factor
    return (in_grad, update)
```

```python
import math

import jax
import jax.numpy as jnp
from jax import lax
from jax.experimental import pallas as pl
from jax.experimental.pallas import tpu as pltpu
from jax.sharding import PartitionSpec as P

damping = 0.1
clip_rate = 0.05
TAPS = 27
F32 = jnp.float32
BF16 = jnp.bfloat16
HI = lax.Precision.HIGHEST
VMEM = pl.BlockSpec(memory_space=pltpu.VMEM)
PARAMS = pltpu.CompilerParams(vmem_limit_bytes=48 * 1024 * 1024)

ORDER = 432
EDGES = (0, 128, 256, 384)
STARTS = (0, 432, 736, 912)
GRAD_AT = 960
COT_AT = 1392
PACKED = 1536


def call(body, out_shape, scratch=(), name=None):
    def run(*args):
        return pl.pallas_call(
            body,
            out_shape=out_shape,
            in_specs=[VMEM] * len(args),
            out_specs=jax.tree.map(lambda _: VMEM, out_shape),
            scratch_shapes=list(scratch),
            compiler_params=PARAMS,
            name=name,
        )(*args)

    return run


def nt(a, b, precision=None):
    return lax.dot_general(a, b, (((1,), (1,)), ((), ())), precision=precision, preferred_element_type=F32)


def nn(a, b, precision=None):
    return lax.dot_general(a, b, (((1,), (0,)), ((), ())), precision=precision, preferred_element_type=F32)


def tn(a, b, precision=None):
    return lax.dot_general(a, b, (((0,), (0,)), ((), ())), precision=precision, preferred_element_type=F32)


def prep_kernel(act_ref, cot_ref, send_ref):
    act = act_ref[...].astype(F32).T.astype(BF16)
    cot = cot_ref[...].astype(F32).T.astype(BF16)
    groups = send_ref.shape[0]
    width = act.shape[0] // groups
    for j in range(groups):
        send_ref[j, 0:width, :] = act[j * width : (j + 1) * width]
        send_ref[j, width:, :] = cot


def in_grad_kernel(prev_ref, cot_ref, next_ref, kern_ref, out_ref, rows_ref, shift_ref):
    rows_ref[8:264, :] = prev_ref[...].astype(F32)
    rows_ref[264:776, :] = cot_ref[...].astype(F32)
    rows_ref[776:1032, :] = next_ref[...].astype(F32)
    z = lax.broadcasted_iota(jnp.int32, (256, 128), 0) % 16
    zeros = jnp.zeros((16, 384), BF16)
    for plane in range(4):
        base = plane * 288
        shift_ref[base : base + 16, :] = zeros
        shift_ref[base + 272 : base + 288, :] = zeros
        for n, c in enumerate((-1, 0, 1)):
            at = 8 + plane * 256 + c
            cells = rows_ref[at : at + 256, :]
            if c:
                cells = jnp.where((z + c >= 0) & (z + c < 16), cells, 0.0)
            shift_ref[base + 16 : base + 272, n * 128 : (n + 1) * 128] = cells.astype(BF16)
    for x in range(2):
        total = jnp.zeros((256, 128), F32)
        for a in (-1, 0, 1):
            for b in (-1, 0, 1):
                for n, c in enumerate((-1, 0, 1)):
                    tap = 9 * (1 - a) + 3 * (1 - b) + (1 - c)
                    at = (x + 1 + a) * 288 + 16 + 16 * b
                    rows = shift_ref[at : at + 256, n * 128 : (n + 1) * 128]
                    total = total + nt(rows, kern_ref[tap])
        out_ref[x * 256 : (x + 1) * 256, :] = total.astype(BF16)


def stats_kernel(recv_ref, prev_ref, next_ref, out_ref, x_ref):
    slabs = recv_ref.shape[0]
    lane = lax.broadcasted_iota(jnp.int32, (16, 1024), 1)
    y = (lane // 16) % 16
    z = lane % 16
    for s in range(slabs):
        cols = slice(s * 512, (s + 1) * 512)
        planes = jnp.concatenate([prev_ref[s], recv_ref[s, 0:16, :], next_ref[s]], axis=1).astype(F32)
        for b in (-1, 0, 1):
            for c in (-1, 0, 1):
                d = 16 * b + c
                moved = planes
                if d:
                    moved = pltpu.roll(planes, (-d) % 1024, 1)
                    ok = (y + b >= 0) & (y + b < 16) & (z + c >= 0) & (z + c < 16)
                    moved = jnp.where(ok, moved, 0.0)
                moved = moved.astype(BF16)
                for a in (-1, 0, 1):
                    tap = 9 * (a + 1) + 3 * (b + 1) + (c + 1)
                    at = (1 + a) * 256
                    x_ref[tap * 16 : (tap + 1) * 16, cols] = moved[:, at : at + 512]
        x_ref[ORDER:, cols] = recv_ref[s, 16:, :]
    for edge, start in zip(EDGES, STARTS):
        tile = nt(x_ref[edge:ORDER, :], x_ref[edge : edge + 128, :])
        out_ref[start : start + ORDER - edge, :] = tile
    out_ref[GRAD_AT : GRAD_AT + ORDER + 128, :] = nt(x_ref[...], x_ref[ORDER:, :])
    out_ref[GRAD_AT + ORDER + 128 :, :] = jnp.zeros((PACKED - GRAD_AT - ORDER - 128, 128), F32)


def spread(row):
    return jnp.broadcast_to(row, (8, 128))


def invert(tiles):
    count = len(tiles)
    lane = lax.broadcasted_iota(jnp.int32, (8, 128), 1)
    sub = lax.broadcasted_iota(jnp.int32, (8, 128), 0)
    tiles = list(tiles)
    for g in range(count):
        rows = tiles[g]
        cols = [jnp.broadcast_to(rows[:, 8 * g + q : 8 * g + q + 1], (8, 128)) for q in range(8)]
        for k in range(8):
            pivot = 1.0 / spread(cols[k][k : k + 1, :])
            scaled = cols[k] * pivot
            for q in range(8):
                if q != k:
                    head = spread(cols[q][k : k + 1, :])
                    cols[q] = jnp.where(sub == k, head * pivot, cols[q] - scaled * head)
            cols[k] = jnp.where(sub == k, pivot, -scaled)
        swept = cols[0] * spread(rows[0:1, :])
        for q in range(1, 8):
            swept = swept + cols[q] * spread(rows[q : q + 1, :])
        for q in range(8):
            swept = jnp.where(lane == 8 * g + q, -cols[q], swept)
        heads = [spread(swept[q : q + 1, :]) for q in range(8)]
        inside = (lane >= 8 * g) & (lane < 8 * g + 8)
        for i in range(count):
            if i == g:
                continue
            old = tiles[i]
            new = jnp.where(inside, 0.0, old)
            for q in range(8):
                new = new - jnp.broadcast_to(old[:, 8 * g + q : 8 * g + q + 1], (8, 128)) * heads[q]
            tiles[i] = new
        tiles[g] = swept
    return [-t for t in tiles]


def solve_kernel(stat_ref, raw_ref, part_ref, d_ref, w_ref, t_ref, b_ref, *, count):
    eye = (
        lax.broadcasted_iota(jnp.int32, (128, 128), 0) == lax.broadcasted_iota(jnp.int32, (128, 128), 1)
    ).astype(F32)

    def tile(p):
        edge = EDGES[p]
        rows = stat_ref[STARTS[p] : STARTS[p] + ORDER - edge, :] / count
        if p == 3:
            rows = jnp.where(lax.broadcasted_iota(jnp.int32, rows.shape, 1) < ORDER - edge, rows, 0.0)
        head = min(128, ORDER - edge)
        first = rows[:head] + damping * eye[:head]
        return jnp.concatenate([first, rows[head:]], axis=0) if head < rows.shape[0] else first

    t = [tile(p) for p in range(4)]
    scaled = stat_ref[GRAD_AT : GRAD_AT + ORDER, :] / math.sqrt(count)
    right = stat_ref[COT_AT : COT_AT + 128, :] / count + damping * eye
    for p in range(4):
        t_ref[STARTS[p] : STARTS[p] + ORDER - EDGES[p], :] = t[p]
    b_ref[...] = scaled

    d_ref[0] = right
    d_ref[1] = t[0][:128]
    for p in range(5):
        m = d_ref[p]
        size = 128 if p < 4 else ORDER - EDGES[3]
        inv = invert([m[8 * i : 8 * i + 8] for i in range(size // 8)])
        for i in range(size // 8):
            w_ref[p, 8 * i : 8 * i + 8, :] = inv[i]
        if 1 <= p < 4:
            q = p - 1
            edge = EDGES[q]
            below = t_ref[STARTS[q] + 128 : STARTS[q] + ORDER - edge, :]
            y = nn(below, w_ref[p], HI)
            t_ref[STARTS[q] + 128 : STARTS[q] + ORDER - edge, :] = y
            b_ref[edge + 128 :, :] = b_ref[edge + 128 :, :] - nn(y, b_ref[edge : edge + 128, :], HI)
            for r in range(q + 1, 4):
                lo = EDGES[r] - EDGES[q] - 128
                head = min(128, ORDER - EDGES[r])
                part = below[lo : lo + head]
                if head < 128:
                    part = jnp.concatenate([part, jnp.zeros((128 - head, 128), F32)], axis=0)
                span = slice(STARTS[r], STARTS[r] + ORDER - EDGES[r])
                new = t_ref[span, :] - nt(y[lo:], part, HI)
                t_ref[span, :] = new
                if r == q + 1:
                    d_ref[p + 1, 0:head, :] = new[:head]
    x3 = nn(w_ref[4, 0:48, 0:48], b_ref[384:432, :], HI)
    raw_ref[384:432, :] = x3
    for q in (2, 1, 0):
        edge = EDGES[q]
        y = t_ref[STARTS[q] + 128 : STARTS[q] + ORDER - edge, :]
        x = nn(w_ref[q + 1], b_ref[edge : edge + 128, :], HI) - tn(y, raw_ref[edge + 128 :, :], HI)
        raw_ref[edge : edge + 128, :] = x
    raw = nn(raw_ref[...], w_ref[0], HI)
    raw_ref[...] = raw
    prod = raw * (stat_ref[GRAD_AT : GRAD_AT + ORDER, :] / math.sqrt(count))
    acc = prod[0:8]
    for i in range(1, ORDER // 8):
        acc = acc + prod[8 * i : 8 * i + 8]
    part_ref[...] = jnp.broadcast_to(jnp.sum(acc).reshape(1, 1), (8, 128))


def on_device(activations, out_grad, kernel):
    shape = activations.shape
    spaces = lax.axis_size("space")
    groups = lax.axis_size("fac")
    act = activations.reshape(512, 128)
    cot = out_grad.reshape(512, 128)
    up = [(i, i + 1) for i in range(spaces - 1)]
    down = [(i + 1, i) for i in range(spaces - 1)]

    cot_prev = lax.ppermute(cot[256:], "space", up)
    cot_next = lax.ppermute(cot[:256], "space", down)

    send = call(prep_kernel, jax.ShapeDtypeStruct((groups, 144, 512), BF16), name="prep")(act, cot)
    recv = lax.all_to_all(send, "fac", 0, 0, tiled=True)
    act_prev = lax.ppermute(recv[:, :16, 256:], "space", up)
    act_next = lax.ppermute(recv[:, :16, :256], "space", down)

    in_grad = call(
        in_grad_kernel,
        jax.ShapeDtypeStruct((512, 128), BF16),
        scratch=[pltpu.VMEM((1040, 128), F32), pltpu.VMEM((1152, 384), BF16)],
        name="in_grad",
    )(cot_prev, cot, cot_next, kernel)

    stats = call(
        stats_kernel,
        jax.ShapeDtypeStruct((PACKED, 128), F32),
        scratch=[pltpu.VMEM((ORDER + 128, groups * 512), BF16)],
        name="stats",
    )(recv, act_prev, act_next)

    share = PACKED // spaces
    parts = lax.all_to_all(stats.reshape(spaces, share, 128), "space", 0, 0, tiled=True)
    mine = jnp.sum(parts, axis=0)
    whole = lax.all_to_all(jnp.broadcast_to(mine[None], (spaces, share, 128)), "space", 0, 0, tiled=True)

    count = float(512 * spaces * groups)

    def body(*refs):
        solve_kernel(*refs, count=count)

    raw, part = call(
        body,
        (jax.ShapeDtypeStruct((ORDER, 128), F32), jax.ShapeDtypeStruct((8, 128), F32)),
        scratch=[
            pltpu.VMEM((5, 128, 128), F32),
            pltpu.VMEM((5, 128, 128), F32),
            pltpu.VMEM((960, 128), F32),
            pltpu.VMEM((ORDER, 128), F32),
        ],
        name="solve",
    )(whole.reshape(PACKED, 128))
    total = part
    for bit in (1, 2, 4):
        total = total + lax.ppermute(total, "fac", [(i, i ^ bit) for i in range(groups)])
    factor = jnp.sqrt(clip_rate * kernel.size / total[0, 0])
    update = raw.reshape(TAPS, 16, 128) * factor
    return (in_grad.reshape(shape), update)


def solution(mesh):
    placed = (P("fac", "space", None, None, None), P("fac", "space", None, None, None), P())
    return jax.shard_map(
        on_device,
        mesh=mesh,
        in_specs=placed,
        out_specs=(P("fac", "space", None, None, None), P(None, "fac", None)),
        check_vma=False,
    )
```

```python
import functools
import math

import jax
import jax.numpy as jnp
from jax import lax
from jax.experimental import pallas as pl
from jax.experimental.pallas import tpu as pltpu
from jax.sharding import PartitionSpec as P

damping = 0.1
clip_rate = 0.05
TAPS = 27
F32 = jnp.float32
BF16 = jnp.bfloat16
HI = lax.Precision.HIGHEST
VMEM = pl.BlockSpec(memory_space=pltpu.VMEM)
PARAMS = pltpu.CompilerParams(vmem_limit_bytes=48 * 1024 * 1024)

ORDER = 432
EDGES = (0, 128, 256, 384)
STARTS = (0, 432, 736, 912)
GRAD_AT = 960
COT_AT = 1392
PACKED = 1536
HALF = PACKED // 2


SMEM = pl.BlockSpec(memory_space=pltpu.SMEM)


def call(body, out_shape, scratch=(), name=None):
    def run(*args):
        return pl.pallas_call(
            body,
            out_shape=out_shape,
            in_specs=[SMEM if a.dtype == jnp.int32 else VMEM for a in args],
            out_specs=jax.tree.map(lambda _: VMEM, out_shape),
            scratch_shapes=list(scratch),
            compiler_params=PARAMS,
            name=name,
        )(*args)

    return run


def nt(a, b, precision=None):
    return lax.dot_general(a, b, (((1,), (1,)), ((), ())), precision=precision, preferred_element_type=F32)


def nn(a, b, precision=None):
    return lax.dot_general(a, b, (((1,), (0,)), ((), ())), precision=precision, preferred_element_type=F32)


def tn(a, b, precision=None):
    return lax.dot_general(a, b, (((0,), (0,)), ((), ())), precision=precision, preferred_element_type=F32)


def prep_kernel(high_ref, act_ref, cot_ref, keep_ref, give_ref, act_t):
    half = act_ref.shape[1] // 2
    act_t[...] = act_ref[...].astype(F32).T.astype(BF16)
    cot = cot_ref[...].astype(F32).T.astype(BF16)
    high = high_ref[0]
    keep_ref[0:half, :] = act_t[pl.ds(pl.multiple_of(high * half, half), half), :]
    give_ref[0:half, :] = act_t[pl.ds(pl.multiple_of((1 - high) * half, half), half), :]
    keep_ref[half:, :] = cot
    give_ref[half:, :] = cot


def spread_kernel(keep_ref, got_ref, send_ref):
    peers = send_ref.shape[0]
    for n, ref in enumerate((keep_ref, got_ref)):
        for p in range(peers):
            send_ref[p, n, 0:16, :] = ref[16 * p : 16 * p + 16, :]
            send_ref[p, n, 16:, :] = ref[16 * peers :, :]


def in_grad_kernel(prev_ref, cot_ref, next_ref, kern_ref, out_ref, rows_ref, shift_ref):
    rows_ref[8:264, :] = prev_ref[...].astype(F32)
    rows_ref[264:776, :] = cot_ref[...].astype(F32)
    rows_ref[776:1032, :] = next_ref[...].astype(F32)
    z = lax.broadcasted_iota(jnp.int32, (256, 128), 0) % 16
    zeros = jnp.zeros((16, 384), BF16)
    for plane in range(4):
        base = plane * 288
        shift_ref[base : base + 16, :] = zeros
        shift_ref[base + 272 : base + 288, :] = zeros
        for n, c in enumerate((-1, 0, 1)):
            at = 8 + plane * 256 + c
            cells = rows_ref[at : at + 256, :]
            if c:
                cells = jnp.where((z + c >= 0) & (z + c < 16), cells, 0.0)
            shift_ref[base + 16 : base + 272, n * 128 : (n + 1) * 128] = cells.astype(BF16)
    for x in range(2):
        total = jnp.zeros((256, 128), F32)
        for a in (-1, 0, 1):
            for b in (-1, 0, 1):
                for n, c in enumerate((-1, 0, 1)):
                    tap = 9 * (1 - a) + 3 * (1 - b) + (1 - c)
                    at = (x + 1 + a) * 288 + 16 + 16 * b
                    rows = shift_ref[at : at + 256, n * 128 : (n + 1) * 128]
                    total = total + nt(rows, kern_ref[tap])
        out_ref[x * 256 : (x + 1) * 256, :] = total.astype(BF16)


def stats_kernel(core_ref, recv_ref, prev_ref, next_ref, out_ref, x_ref):
    core = core_ref[0]
    slots = (core, 1 - core)

    def store(start, value):
        stop = start + value.shape[0]
        for h in range(2):
            lo, hi = max(start, h * HALF), min(stop, (h + 1) * HALF)
            if lo < hi:
                out_ref[slots[h], lo - h * HALF : hi - h * HALF, :] = value[lo - start : hi - start]

    slabs = recv_ref.shape[0]
    lane = lax.broadcasted_iota(jnp.int32, (16, 1024), 1)
    y = (lane // 16) % 16
    z = lane % 16
    for s in range(slabs):
        cols = slice(s * 512, (s + 1) * 512)
        planes = jnp.concatenate([prev_ref[s], recv_ref[s, 0:16, :], next_ref[s]], axis=1).astype(F32)
        for b in (-1, 0, 1):
            for c in (-1, 0, 1):
                d = 16 * b + c
                moved = planes
                if d:
                    moved = pltpu.roll(planes, (-d) % 1024, 1)
                    ok = (y + b >= 0) & (y + b < 16) & (z + c >= 0) & (z + c < 16)
                    moved = jnp.where(ok, moved, 0.0)
                moved = moved.astype(BF16)
                for a in (-1, 0, 1):
                    tap = 9 * (a + 1) + 3 * (b + 1) + (c + 1)
                    at = (1 + a) * 256
                    x_ref[tap * 16 : (tap + 1) * 16, cols] = moved[:, at : at + 512]
        x_ref[ORDER:, cols] = recv_ref[s, 16:, :]
    for edge, start in zip(EDGES, STARTS):
        tile = nt(x_ref[edge:ORDER, :], x_ref[edge : edge + 128, :])
        store(start, tile)
    store(GRAD_AT, nt(x_ref[...], x_ref[ORDER:, :]))
    store(COT_AT + 128, jnp.zeros((PACKED - COT_AT - 128, 128), F32))


def fold_kernel(parts_ref, out_ref):
    peers = parts_ref.shape[0]
    total = parts_ref[0]
    for p in range(1, peers):
        total = total + parts_ref[p]
    for p in range(peers):
        out_ref[p] = total


def scale_kernel(raw_ref, parts_ref, out_ref, *, size):
    total = parts_ref[0]
    for p in range(1, parts_ref.shape[0]):
        total = total + parts_ref[p]
    factor = jnp.sqrt(clip_rate * size / total)[0:1, :]
    out_ref[...] = raw_ref[...] * factor


def spread(row):
    return jnp.broadcast_to(row, (8, 128))


def sweep(tiles, g):
    lane = lax.broadcasted_iota(jnp.int32, (8, 128), 1)
    sub = lax.broadcasted_iota(jnp.int32, (8, 128), 0)
    rows = tiles[g]
    cols = [jnp.broadcast_to(rows[:, 8 * g + q : 8 * g + q + 1], (8, 128)) for q in range(8)]
    for k in range(8):
        pivot = 1.0 / spread(cols[k][k : k + 1, :])
        scaled = cols[k] * pivot
        for q in range(8):
            if q != k:
                head = spread(cols[q][k : k + 1, :])
                cols[q] = jnp.where(sub == k, head * pivot, cols[q] - scaled * head)
        cols[k] = jnp.where(sub == k, pivot, -scaled)
    swept = cols[0] * spread(rows[0:1, :])
    for q in range(1, 8):
        swept = swept + cols[q] * spread(rows[q : q + 1, :])
    for q in range(8):
        swept = jnp.where(lane == 8 * g + q, -cols[q], swept)
    heads = [spread(swept[q : q + 1, :]) for q in range(8)]
    inside = (lane >= 8 * g) & (lane < 8 * g + 8)
    out = []
    for i, old in enumerate(tiles):
        if i == g:
            out.append(swept)
            continue
        new = jnp.where(inside, 0.0, old)
        for q in range(8):
            new = new - jnp.broadcast_to(old[:, 8 * g + q : 8 * g + q + 1], (8, 128)) * heads[q]
        out.append(new)
    return out


def invert(*mats):
    held = [[m[8 * i : 8 * i + 8] for i in range(m.shape[0] // 8)] for m in mats]
    for g in range(len(held[0])):
        held = [sweep(tiles, g) for tiles in held]
    return [[-t for t in tiles] for tiles in held]


def solve_kernel(core_ref, mine_ref, other_ref, raw_ref, part_ref, stat_ref, d_ref, w_ref, t_ref, b_ref, *, count):
    core = core_ref[0]
    stat_ref[pl.ds(pl.multiple_of(core * HALF, HALF), HALF), :] = mine_ref[...]
    stat_ref[pl.ds(pl.multiple_of((1 - core) * HALF, HALF), HALF), :] = other_ref[...]
    eye = (
        lax.broadcasted_iota(jnp.int32, (128, 128), 0) == lax.broadcasted_iota(jnp.int32, (128, 128), 1)
    ).astype(F32)

    def tile(p):
        edge = EDGES[p]
        rows = stat_ref[STARTS[p] : STARTS[p] + ORDER - edge, :] / count
        if p == 3:
            rows = jnp.where(lax.broadcasted_iota(jnp.int32, rows.shape, 1) < ORDER - edge, rows, 0.0)
        head = min(128, ORDER - edge)
        first = rows[:head] + damping * eye[:head]
        return jnp.concatenate([first, rows[head:]], axis=0) if head < rows.shape[0] else first

    t = [tile(p) for p in range(4)]
    scaled = stat_ref[GRAD_AT : GRAD_AT + ORDER, :] / math.sqrt(count)
    right = stat_ref[COT_AT : COT_AT + 128, :] / count + damping * eye
    for p in range(4):
        t_ref[STARTS[p] : STARTS[p] + ORDER - EDGES[p], :] = t[p]
    b_ref[...] = scaled

    d_ref[0] = right
    d_ref[1] = t[0][:128]
    for p in range(1, 5):
        size = 128 if p < 4 else ORDER - EDGES[3]
        at = (0, 1) if p == 1 else (p,)
        for n, inv in zip(at, invert(*[d_ref[n, 0:size, :] for n in at])):
            for i in range(size // 8):
                w_ref[n, 8 * i : 8 * i + 8, :] = inv[i]
        if p < 4:
            q = p - 1
            edge = EDGES[q]
            below = t_ref[STARTS[q] + 128 : STARTS[q] + ORDER - edge, :]
            y = nn(below, w_ref[p], HI)
            t_ref[STARTS[q] + 128 : STARTS[q] + ORDER - edge, :] = y
            b_ref[edge + 128 :, :] = b_ref[edge + 128 :, :] - nn(y, b_ref[edge : edge + 128, :], HI)
            for r in range(q + 1, 4):
                lo = EDGES[r] - EDGES[q] - 128
                head = min(128, ORDER - EDGES[r])
                part = below[lo : lo + head]
                if head < 128:
                    part = jnp.concatenate([part, jnp.zeros((128 - head, 128), F32)], axis=0)
                span = slice(STARTS[r], STARTS[r] + ORDER - EDGES[r])
                new = t_ref[span, :] - nt(y[lo:], part, HI)
                t_ref[span, :] = new
                if r == q + 1:
                    d_ref[p + 1, 0:head, :] = new[:head]
    x3 = nn(w_ref[4, 0:48, 0:48], b_ref[384:432, :], HI)
    raw_ref[384:432, :] = x3
    for q in (2, 1, 0):
        edge = EDGES[q]
        y = t_ref[STARTS[q] + 128 : STARTS[q] + ORDER - edge, :]
        x = nn(w_ref[q + 1], b_ref[edge : edge + 128, :], HI) - tn(y, raw_ref[edge + 128 :, :], HI)
        raw_ref[edge : edge + 128, :] = x
    raw = nn(raw_ref[...], w_ref[0], HI)
    raw_ref[...] = raw
    prod = raw * (stat_ref[GRAD_AT : GRAD_AT + ORDER, :] / math.sqrt(count))
    acc = prod[0:8]
    for i in range(1, ORDER // 8):
        acc = acc + prod[8 * i : 8 * i + 8]
    part_ref[...] = jnp.broadcast_to(jnp.sum(acc).reshape(1, 1, 1), part_ref.shape)


def on_device(activations, out_grad, kernel):
    shape = activations.shape
    spaces = lax.axis_size("space")
    groups = lax.axis_size("fac")
    act = activations.reshape(512, 128)
    cot = out_grad.reshape(512, 128)
    up = [(i, i + 1) for i in range(spaces - 1)]
    down = [(i + 1, i) for i in range(spaces - 1)]

    cot_prev = lax.ppermute(cot[256:], "space", up)
    cot_next = lax.ppermute(cot[:256], "space", down)

    wide = groups // 2
    high = (lax.axis_index("fac") // wide).astype(jnp.int32).reshape(1)
    core = (lax.axis_index("space") % 2).astype(jnp.int32).reshape(1)
    keep, give = call(
        prep_kernel,
        (jax.ShapeDtypeStruct((192, 512), BF16),) * 2,
        scratch=[pltpu.VMEM((128, 512), BF16)],
        name="prep",
    )(high, act, cot)
    got = lax.ppermute(give, "fac", [(i, (i + wide) % groups) for i in range(groups)])
    send = call(spread_kernel, jax.ShapeDtypeStruct((wide, 2, 144, 512), BF16), name="spread")(keep, got)
    along_x = [[h * wide + x for x in range(wide)] for h in range(2)]
    recv = lax.all_to_all(send, "fac", 0, 0, axis_index_groups=along_x, tiled=True).reshape(groups, 144, 512)
    act_prev = lax.ppermute(recv[:, :16, 256:], "space", up)
    act_next = lax.ppermute(recv[:, :16, :256], "space", down)

    in_grad = call(
        in_grad_kernel,
        jax.ShapeDtypeStruct((512, 128), BF16),
        scratch=[pltpu.VMEM((1040, 128), F32), pltpu.VMEM((1152, 384), BF16)],
        name="in_grad",
    )(cot_prev, cot, cot_next, kernel)

    stats = call(
        stats_kernel,
        jax.ShapeDtypeStruct((2, HALF, 128), F32),
        scratch=[pltpu.VMEM((ORDER + 128, groups * 512), BF16)],
        name="stats",
    )(core, recv, act_prev, act_next)

    swap = [(i, i ^ 1) for i in range(spaces)]
    chips = spaces // 2
    share = HALF // chips
    plane = [[2 * i + c for i in range(chips)] for c in range(2)]
    both = stats[0] + lax.ppermute(stats[1], "space", swap)
    parts = lax.all_to_all(
        both.reshape(chips, share, 128), "space", 0, 0, axis_index_groups=plane, tiled=True
    )
    copies = call(fold_kernel, jax.ShapeDtypeStruct((chips, share, 128), F32), name="fold")(parts)
    mine = lax.all_to_all(copies, "space", 0, 0, axis_index_groups=plane, tiled=True).reshape(HALF, 128)
    other = lax.ppermute(mine, "space", swap)

    raw, part = call(
        functools.partial(solve_kernel, count=float(512 * spaces * groups)),
        (jax.ShapeDtypeStruct((ORDER, 128), F32), jax.ShapeDtypeStruct((groups, 8, 128), F32)),
        scratch=[
            pltpu.VMEM((PACKED, 128), F32),
            pltpu.VMEM((5, 128, 128), F32),
            pltpu.VMEM((5, 128, 128), F32),
            pltpu.VMEM((960, 128), F32),
            pltpu.VMEM((ORDER, 128), F32),
        ],
        name="solve",
    )(core, mine, other)
    every = lax.all_to_all(part, "fac", 0, 0, tiled=True)
    update = call(
        functools.partial(scale_kernel, size=kernel.size),
        jax.ShapeDtypeStruct((ORDER, 128), F32),
        name="scale",
    )(raw, every)
    return (in_grad.reshape(shape), update.reshape(TAPS, 16, 128))


def solution(mesh):
    placed = (P("fac", "space", None, None, None), P("fac", "space", None, None, None), P())
    return jax.shard_map(
        on_device,
        mesh=mesh,
        in_specs=placed,
        out_specs=(P("fac", "space", None, None, None), P(None, "fac", None)),
        check_vma=False,
    )
```

```python
import functools
import math

import jax
import jax.numpy as jnp
from jax import lax
from jax.experimental import pallas as pl
from jax.experimental.pallas import tpu as pltpu
from jax.sharding import PartitionSpec as P

damping = 0.1
clip_rate = 0.05
TAPS = 27
F32 = jnp.float32
BF16 = jnp.bfloat16
HI = lax.Precision.HIGHEST
VMEM = pl.BlockSpec(memory_space=pltpu.VMEM)
PARAMS = pltpu.CompilerParams(vmem_limit_bytes=48 * 1024 * 1024)

ORDER = 432
EDGES = (0, 128, 256, 384)
STARTS = (0, 432, 736, 912)
GRAD_AT = 960
COT_AT = 1392
PACKED = 1536
HALF = PACKED // 2
QUARTER = HALF // 4


SMEM = pl.BlockSpec(memory_space=pltpu.SMEM)


def call(body, out_shape, scratch=(), name=None):
    def run(*args):
        return pl.pallas_call(
            body,
            out_shape=out_shape,
            in_specs=[SMEM if a.dtype == jnp.int32 else VMEM for a in args],
            out_specs=jax.tree.map(lambda _: VMEM, out_shape),
            scratch_shapes=list(scratch),
            compiler_params=PARAMS,
            name=name,
        )(*args)

    return run


def nt(a, b, precision=None):
    return lax.dot_general(a, b, (((1,), (1,)), ((), ())), precision=precision, preferred_element_type=F32)


def nn(a, b, precision=None):
    return lax.dot_general(a, b, (((1,), (0,)), ((), ())), precision=precision, preferred_element_type=F32)


def tn(a, b, precision=None):
    return lax.dot_general(a, b, (((0,), (0,)), ((), ())), precision=precision, preferred_element_type=F32)


def prep_kernel(place_ref, act_ref, cot_ref, give_ref, *rest):
    sends, act_t = rest[:-1], rest[-1]
    half = act_ref.shape[1] // 2
    act_t[...] = act_ref[...].astype(F32).T.astype(BF16)
    cot = cot_ref[...].astype(F32).T.astype(BF16)
    high, turn = place_ref[2], place_ref[3]
    give_ref[0:half, :] = act_t[pl.ds(pl.multiple_of((1 - high) * half, half), half), :]
    give_ref[half:, :] = cot
    for k, send_ref in enumerate(sends):
        at = high * half + ((turn + k) % 4) * 16
        send_ref[0:16, :] = act_t[pl.ds(pl.multiple_of(at, 16), 16), :]
        send_ref[16:, :] = cot


def spread_kernel(place_ref, got_ref, *sends):
    half = got_ref.shape[0] - 128
    for k, send_ref in enumerate(sends):
        at = ((place_ref[3] + k) % 4) * 16
        send_ref[0:16, :] = got_ref[pl.ds(pl.multiple_of(at, 16), 16), :]
        send_ref[16:, :] = got_ref[half:, :]


def rim_kernel(*refs):
    parts, (first_ref, last_ref) = refs[:-2], refs[-2:]
    for s, ref in enumerate(parts):
        first_ref[s] = ref[0:16, 0:256]
        last_ref[s] = ref[0:16, 256:]


def in_grad_kernel(prev_ref, cot_ref, next_ref, kern_ref, out_ref, rows_ref, shift_ref):
    rows_ref[8:264, :] = prev_ref[...].astype(F32)
    rows_ref[264:776, :] = cot_ref[...].astype(F32)
    rows_ref[776:1032, :] = next_ref[...].astype(F32)
    z = lax.broadcasted_iota(jnp.int32, (256, 128), 0) % 16
    zeros = jnp.zeros((16, 384), BF16)
    for plane in range(4):
        base = plane * 288
        shift_ref[base : base + 16, :] = zeros
        shift_ref[base + 272 : base + 288, :] = zeros
        for n, c in enumerate((-1, 0, 1)):
            at = 8 + plane * 256 + c
            cells = rows_ref[at : at + 256, :]
            if c:
                cells = jnp.where((z + c >= 0) & (z + c < 16), cells, 0.0)
            shift_ref[base + 16 : base + 272, n * 128 : (n + 1) * 128] = cells.astype(BF16)
    for x in range(2):
        total = jnp.zeros((256, 128), F32)
        for a in (-1, 0, 1):
            for b in (-1, 0, 1):
                for n, c in enumerate((-1, 0, 1)):
                    tap = 9 * (1 - a) + 3 * (1 - b) + (1 - c)
                    at = (x + 1 + a) * 288 + 16 + 16 * b
                    rows = shift_ref[at : at + 256, n * 128 : (n + 1) * 128]
                    total = total + nt(rows, kern_ref[tap])
        out_ref[x * 256 : (x + 1) * 256, :] = total.astype(BF16)


def stats_kernel(place_ref, prev_ref, next_ref, *refs):
    slabs = prev_ref.shape[0]
    parts, (keep_ref, give_ref, x_ref, out_ref) = refs[:slabs], refs[slabs:]
    core, turn = place_ref[0], place_ref[1]
    lane = lax.broadcasted_iota(jnp.int32, (16, 1024), 1)
    y = (lane // 16) % 16
    z = lane % 16
    for s in range(slabs):
        cols = slice(s * 512, (s + 1) * 512)
        planes = jnp.concatenate([prev_ref[s], parts[s][0:16, :], next_ref[s]], axis=1).astype(F32)
        for b in (-1, 0, 1):
            for c in (-1, 0, 1):
                d = 16 * b + c
                moved = planes
                if d:
                    moved = pltpu.roll(planes, (-d) % 1024, 1)
                    ok = (y + b >= 0) & (y + b < 16) & (z + c >= 0) & (z + c < 16)
                    moved = jnp.where(ok, moved, 0.0)
                moved = moved.astype(BF16)
                for a in (-1, 0, 1):
                    tap = 9 * (a + 1) + 3 * (b + 1) + (c + 1)
                    at = (1 + a) * 256
                    x_ref[tap * 16 : (tap + 1) * 16, cols] = moved[:, at : at + 512]
        x_ref[ORDER:, cols] = parts[s][16:, :]
    for edge, start in zip(EDGES, STARTS):
        tile = nt(x_ref[edge:ORDER, :], x_ref[edge : edge + 128, :])
        out_ref[start : start + ORDER - edge, :] = tile
    out_ref[GRAD_AT : GRAD_AT + ORDER + 128, :] = nt(x_ref[...], x_ref[ORDER:, :])
    out_ref[COT_AT + 128 :, :] = jnp.zeros((PACKED - COT_AT - 128, 128), F32)
    for k in range(4):
        for half, ref in ((core, keep_ref), (1 - core, give_ref)):
            at = half * HALF + ((turn + k) % 4) * QUARTER
            ref[k * QUARTER : (k + 1) * QUARTER, :] = out_ref[pl.ds(pl.multiple_of(at, QUARTER), QUARTER), :]


def pair_kernel(keep_ref, got_ref, *outs):
    for k, out_ref in enumerate(outs):
        rows = slice(k * QUARTER, (k + 1) * QUARTER)
        out_ref[...] = keep_ref[rows, :] + got_ref[rows, :]


def fold_kernel(*refs):
    total = refs[0][...]
    for ref in refs[1:-1]:
        total = total + ref[...]
    refs[-1][...] = total


def fold_in_order_kernel(place_ref, *refs):
    parts, out_ref, slots = refs[:4], refs[4], refs[5]
    for k, ref in enumerate(parts):
        slots[(place_ref[4] + 4 - k) % 4] = ref[...]
    out_ref[...] = slots[0] + slots[1] + slots[2] + slots[3]


def scale_kernel(raw_ref, parts_ref, out_ref, *, size):
    total = parts_ref[0]
    for p in range(1, parts_ref.shape[0]):
        total = total + parts_ref[p]
    factor = jnp.sqrt(clip_rate * size / total)[0:1, :]
    out_ref[...] = raw_ref[...] * factor


def spread(row):
    return jnp.broadcast_to(row, (8, 128))


def sweep(tiles, g):
    shape = tiles[g].shape
    lane = lax.broadcasted_iota(jnp.int32, shape, 1)
    sub = lax.broadcasted_iota(jnp.int32, shape, 0)
    rows = tiles[g]

    def column(tile, q):
        return jnp.broadcast_to(tile[:, 8 * g + q : 8 * g + q + 1], shape)

    def row(tile, q):
        return jnp.broadcast_to(tile[q : q + 1, :], shape)

    cols = [column(rows, q) for q in range(8)]
    for k in range(0, 8, 2):
        one, two = cols[k], cols[k + 1]
        a, b, d = row(one, k), row(one, k + 1), row(two, k + 1)
        scale = 1.0 / (a * d - b * b)
        ia, ib, id_ = d * scale, -b * scale, a * scale
        upper, lower = sub == k, sub == k + 1
        for q in range(8):
            if q in (k, k + 1):
                continue
            h, l = row(cols[q], k), row(cols[q], k + 1)
            th, tl = ia * h + ib * l, ib * h + id_ * l
            rest = cols[q] - one * th - two * tl
            cols[q] = jnp.where(upper, th, jnp.where(lower, tl, rest))
        cols[k] = jnp.where(upper, ia, jnp.where(lower, ib, -(one * ia + two * ib)))
        cols[k + 1] = jnp.where(upper, ib, jnp.where(lower, id_, -(one * ib + two * id_)))
    terms = [cols[q] * row(rows, q) for q in range(8)]
    while len(terms) > 1:
        terms = [x + y for x, y in zip(terms[::2], terms[1::2])]
    swept = terms[0]
    for q in range(8):
        swept = jnp.where(lane == 8 * g + q, -cols[q], swept)
    heads = [row(swept, q) for q in range(8)]
    inside = (lane >= 8 * g) & (lane < 8 * g + 8)
    out = []
    for i, old in enumerate(tiles):
        if i == g:
            out.append(swept)
            continue
        new = jnp.where(inside, 0.0, old)
        for q in range(8):
            new = new - column(old, q) * heads[q]
        out.append(new)
    return out


def invert(*mats):
    held = [[m[8 * i : 8 * i + 8] for i in range(m.shape[0] // 8)] for m in mats]
    for g in range(len(held[0])):
        held = [sweep(tiles, g) for tiles in held]
    return [jnp.concatenate([-t for t in tiles], axis=0) for tiles in held]


STEP = 64
STEPS = tuple(range(0, ORDER, STEP))


def packed(col, row, rows):
    tile = col // 128
    at = STARTS[tile] + row - EDGES[tile]
    return slice(at, at + rows)


def forward_kernel(core_ref, *refs, count):
    mine, others = refs[:4], refs[4:8]
    z_ref, y_ref, right_ref, part_ref, stat_ref, d_ref, b_ref = refs[8:]
    core, turn = core_ref[0], core_ref[1]
    for k in range(4):
        for half, ref in ((core, mine[k]), (1 - core, others[k])):
            at = half * HALF + ((turn + 4 - k) % 4) * QUARTER
            stat_ref[pl.ds(pl.multiple_of(at, QUARTER), QUARTER), :] = ref[...]
    eye = (
        lax.broadcasted_iota(jnp.int32, (128, 128), 0) == lax.broadcasted_iota(jnp.int32, (128, 128), 1)
    ).astype(F32)
    for p in range(4):
        edge = EDGES[p]
        head = min(128, ORDER - edge)
        rows = stat_ref[STARTS[p] : STARTS[p] + ORDER - edge, :] / count
        y_ref[STARTS[p] : STARTS[p] + ORDER - edge, :] = rows
        y_ref[STARTS[p] : STARTS[p] + head, :] = rows[:head] + damping * eye[:head]
    b_ref[...] = stat_ref[GRAD_AT : GRAD_AT + ORDER, :] / math.sqrt(count)
    right = stat_ref[COT_AT : COT_AT + 128, :] / count + damping * eye

    side = right[64:, :64]
    for p, edge in enumerate(STEPS):
        size = min(STEP, ORDER - edge)
        half = (edge % 128) // STEP
        lanes = slice(half * STEP, half * STEP + size)
        d = y_ref[packed(edge, edge, size), lanes] if p == 0 else d_ref[0:size, 0:size]
        if p == 0:
            w, r_inv = invert(d, right[:64, :64])
            r_y = nn(side, r_inv, HI)
            r_next = right[64:, 64:] - nt(r_y, side, HI)
        elif p == 1:
            w, t_inv = invert(d, r_next)
            low = -nn(t_inv, r_y, HI)
            top = r_inv - tn(r_y, low, HI)
            inverse = jnp.concatenate(
                [jnp.concatenate([top, low.T], axis=1), jnp.concatenate([low, t_inv], axis=1)], axis=0
            )
            right_ref[...] = inverse
        else:
            (w,) = invert(d)
        z_ref[edge : edge + size, :] = nn(w, b_ref[edge : edge + size, :], HI)
        below = edge + size
        left = ORDER - below
        if left == 0:
            break
        low = y_ref[packed(edge, below, left), lanes]
        y = nn(low, w, HI)
        near = min(STEP, left)
        at = slice((1 - half) * STEP, (1 - half) * STEP + near)
        d_ref[0:near, 0:near] = y_ref[packed(below, below, near), at] - nt(y[:near], low[:near], HI)
        y_ref[packed(edge, below, left), lanes] = y
        b_ref[below:, :] = b_ref[below:, :] - nn(y, b_ref[edge : edge + size, :], HI)
        if half == 0:
            span = packed(edge, below, left)
            y_ref[span, STEP:] = y_ref[span, STEP:] - nt(y, low[:STEP], HI)
        for tile in range(edge // 128 + 1, 4):
            first = EDGES[tile] - below
            wide = min(128, ORDER - EDGES[tile])
            span = slice(STARTS[tile], STARTS[tile] + ORDER - EDGES[tile])
            y_ref[span, 0:wide] = y_ref[span, 0:wide] - nt(y[first:], low[first : first + wide], HI)
    prod = tn(b_ref[...], z_ref[...], HI) * right_ref[...]
    acc = prod[0:8]
    for i in range(1, 16):
        acc = acc + prod[8 * i : 8 * i + 8]
    part_ref[...] = jnp.broadcast_to(jnp.sum(acc).reshape(1, 1, 1), part_ref.shape)


def backward_kernel(z_ref, y_ref, right_ref, raw_ref, x_ref):
    for edge in reversed(STEPS):
        size = min(STEP, ORDER - edge)
        below = edge + size
        x = z_ref[edge : edge + size, :]
        if below < ORDER:
            lanes = slice(edge % 128, edge % 128 + size)
            y = y_ref[packed(edge, below, ORDER - below), lanes]
            x = x - tn(y, x_ref[below:, :], HI)
        x_ref[edge : edge + size, :] = x
    raw_ref[...] = nn(x_ref[...], right_ref[...], HI)


def on_device(activations, out_grad, kernel):
    shape = activations.shape
    spaces = lax.axis_size("space")
    groups = lax.axis_size("fac")
    wide = groups // 2
    act = activations.reshape(512, 128)
    cot = out_grad.reshape(512, 128)

    sp, fa = lax.axis_index("space"), lax.axis_index("fac")
    place = jnp.stack([sp % 2, sp // 2 % 4, fa // wide, fa % wide, sp // 8]).astype(jnp.int32)
    up = [(i, i + 1) for i in range(spaces - 1)]
    down = [(i + 1, i) for i in range(spaces - 1)]
    swap = [(i, i ^ 1) for i in range(spaces)]
    ends = [(i, (i + wide) % groups) for i in range(groups)]

    def ring_x(k):
        return [(i, i // wide * wide + (i + k) % wide) for i in range(groups)]

    def ring_y(k):
        return [(i, i // 8 * 8 + (i // 2 % 4 + k) % 4 * 2 + i % 2) for i in range(spaces)]

    def ring_z(k):
        return [(i, (i // 8 + k) % 4 * 8 + i % 8) for i in range(spaces)]

    def rows(count, width=128, dtype=F32):
        return jax.ShapeDtypeStruct((count, width), dtype)

    part = rows(144, 512, BF16)
    give, *sends = call(
        prep_kernel,
        (rows(192, 512, BF16),) + (part,) * 4,
        scratch=[pltpu.VMEM((128, 512), BF16)],
        name="prep",
    )(place, act, cot)
    got = lax.ppermute(give, "fac", ends)
    own = [sends[0]] + [lax.ppermute(sends[k], "fac", ring_x(k)) for k in (1, 2, 3)]
    cot_prev = lax.ppermute(cot[256:], "space", up)
    cot_next = lax.ppermute(cot[:256], "space", down)
    got, own, cot_prev, cot_next = lax.optimization_barrier((got, own, cot_prev, cot_next))

    sends = call(spread_kernel, (part,) * 4, name="spread")(place, got)
    far = [sends[0]] + [lax.ppermute(sends[k], "fac", ring_x(k)) for k in (1, 2, 3)]
    in_grad = call(
        in_grad_kernel,
        rows(512, 128, BF16),
        scratch=[pltpu.VMEM((1040, 128), F32), pltpu.VMEM((1152, 384), BF16)],
        name="in_grad",
    )(cot_prev, cot, cot_next, kernel)
    far, in_grad = lax.optimization_barrier((far, in_grad))

    parts = own + far
    first, last = call(rim_kernel, (jax.ShapeDtypeStruct((groups, 16, 256), BF16),) * 2, name="rim")(*parts)
    prev = lax.ppermute(last, "space", up)
    following = lax.ppermute(first, "space", down)

    keep, give = call(
        stats_kernel,
        (rows(HALF),) * 2,
        scratch=[pltpu.VMEM((ORDER + 128, groups * 512), BF16), pltpu.VMEM((PACKED, 128), F32)],
        name="stats",
    )(place, prev, following, *parts)

    got = lax.ppermute(give, "space", swap)
    quarters = call(pair_kernel, (rows(QUARTER),) * 4, name="pair")(keep, got)
    over_y = [lax.ppermute(quarters[k], "space", ring_y(k)) for k in (1, 2, 3)]
    mine = call(fold_kernel, rows(QUARTER), name="fold_y")(quarters[0], *over_y)
    over_z = [lax.ppermute(mine, "space", ring_z(k)) for k in (1, 2, 3)]
    mine = call(
        fold_in_order_kernel,
        rows(QUARTER),
        scratch=[pltpu.VMEM((4, QUARTER, 128), F32)],
        name="fold_z",
    )(place, mine, *over_z)
    mine = [mine] + [lax.ppermute(mine, "space", ring_y(k)) for k in (1, 2, 3)]
    others = [lax.ppermute(q, "space", swap) for q in mine]

    z, y, right, total = call(
        functools.partial(forward_kernel, count=float(512 * spaces * groups)),
        (rows(ORDER), rows(GRAD_AT), rows(128), jax.ShapeDtypeStruct((groups, 8, 128), F32)),
        scratch=[pltpu.VMEM((PACKED, 128), F32), pltpu.VMEM((STEP, STEP), F32), pltpu.VMEM((ORDER, 128), F32)],
        name="forward",
    )(place, *mine, *others)
    every = lax.all_to_all(total, "fac", 0, 0, tiled=True)
    raw = call(backward_kernel, rows(ORDER), scratch=[pltpu.VMEM((ORDER, 128), F32)], name="backward")(z, y, right)
    update = call(functools.partial(scale_kernel, size=kernel.size), rows(ORDER), name="scale")(raw, every)
    return (in_grad.reshape(shape), update.reshape(TAPS, 16, 128))


def solution(mesh):
    placed = (P("fac", "space", None, None, None), P("fac", "space", None, None, None), P())
    return jax.shard_map(
        on_device,
        mesh=mesh,
        in_specs=placed,
        out_specs=(P("fac", "space", None, None, None), P(None, "fac", None)),
        check_vma=False,
    )
```

```python
import functools
import math

import jax
import jax.numpy as jnp
from jax import lax
from jax.experimental import pallas as pl
from jax.experimental.pallas import tpu as pltpu
from jax.sharding import PartitionSpec as P

damping = 0.1
clip_rate = 0.05
TAPS = 27
F32 = jnp.float32
BF16 = jnp.bfloat16
HI = lax.Precision.HIGHEST
VMEM = pl.BlockSpec(memory_space=pltpu.VMEM)
PARAMS = pltpu.CompilerParams(vmem_limit_bytes=48 * 1024 * 1024)

ORDER = 432
EDGES = (0, 128, 256, 384)
STARTS = (0, 432, 736, 912)
GRAD_AT = 960
COT_AT = 1392
PACKED = 1536
HALF = PACKED // 2
QUARTER = HALF // 4


SMEM = pl.BlockSpec(memory_space=pltpu.SMEM)


def call(body, out_shape, scratch=(), name=None):
    def run(*args):
        return pl.pallas_call(
            body,
            out_shape=out_shape,
            in_specs=[SMEM if a.dtype == jnp.int32 else VMEM for a in args],
            out_specs=jax.tree.map(lambda _: VMEM, out_shape),
            scratch_shapes=list(scratch),
            compiler_params=PARAMS,
            name=name,
        )(*args)

    return run


def nt(a, b, precision=None):
    return lax.dot_general(a, b, (((1,), (1,)), ((), ())), precision=precision, preferred_element_type=F32)


def nn(a, b, precision=None):
    return lax.dot_general(a, b, (((1,), (0,)), ((), ())), precision=precision, preferred_element_type=F32)


def tn(a, b, precision=None):
    return lax.dot_general(a, b, (((0,), (0,)), ((), ())), precision=precision, preferred_element_type=F32)


def prep_kernel(place_ref, act_ref, cot_ref, give_ref, *rest):
    sends, act_t = rest[:-1], rest[-1]
    half = act_ref.shape[1] // 2
    act_t[...] = act_ref[...].astype(F32).T.astype(BF16)
    cot = cot_ref[...].astype(F32).T.astype(BF16)
    high, turn = place_ref[2], place_ref[3]
    give_ref[0:half, :] = act_t[pl.ds(pl.multiple_of((1 - high) * half, half), half), :]
    give_ref[half:, :] = cot
    for k, send_ref in enumerate(sends):
        at = high * half + ((turn + k) % 4) * 16
        send_ref[0:16, :] = act_t[pl.ds(pl.multiple_of(at, 16), 16), :]
        send_ref[16:, :] = cot


def spread_kernel(place_ref, got_ref, *sends):
    half = got_ref.shape[0] - 128
    for k, send_ref in enumerate(sends):
        at = ((place_ref[3] + k) % 4) * 16
        send_ref[0:16, :] = got_ref[pl.ds(pl.multiple_of(at, 16), 16), :]
        send_ref[16:, :] = got_ref[half:, :]


def rim_kernel(*refs):
    parts, (first_ref, last_ref) = refs[:-2], refs[-2:]
    for s, ref in enumerate(parts):
        first_ref[16 * s : 16 * s + 16, :] = ref[0:16, 0:256]
        last_ref[16 * s : 16 * s + 16, :] = ref[0:16, 256:]
    first_ref[128:, :] = parts[0][16:, 0:256]
    last_ref[128:, :] = parts[0][16:, 256:]


def in_grad_kernel(prev_ref, cot_ref, next_ref, kern_ref, out_ref, rows_ref, shift_ref):
    rows_ref[8:264, :] = prev_ref[128:, :].astype(F32).T
    rows_ref[264:776, :] = cot_ref[...].astype(F32)
    rows_ref[776:1032, :] = next_ref[128:, :].astype(F32).T
    z = lax.broadcasted_iota(jnp.int32, (256, 128), 0) % 16
    zeros = jnp.zeros((16, 384), BF16)
    for plane in range(4):
        base = plane * 288
        shift_ref[base : base + 16, :] = zeros
        shift_ref[base + 272 : base + 288, :] = zeros
        for n, c in enumerate((-1, 0, 1)):
            at = 8 + plane * 256 + c
            cells = rows_ref[at : at + 256, :]
            if c:
                cells = jnp.where((z + c >= 0) & (z + c < 16), cells, 0.0)
            shift_ref[base + 16 : base + 272, n * 128 : (n + 1) * 128] = cells.astype(BF16)
    for x in range(2):
        total = jnp.zeros((256, 128), F32)
        for a in (-1, 0, 1):
            for b in (-1, 0, 1):
                for n, c in enumerate((-1, 0, 1)):
                    tap = 9 * (1 - a) + 3 * (1 - b) + (1 - c)
                    at = (x + 1 + a) * 288 + 16 + 16 * b
                    rows = shift_ref[at : at + 256, n * 128 : (n + 1) * 128]
                    total = total + nt(rows, kern_ref[tap])
        out_ref[x * 256 : (x + 1) * 256, :] = total.astype(BF16)


def stats_kernel(place_ref, prev_ref, next_ref, *refs, slabs):
    parts, (keep_ref, give_ref, x_ref, out_ref) = refs[:slabs], refs[slabs:]
    core, turn = place_ref[0], place_ref[1]
    lane = lax.broadcasted_iota(jnp.int32, (16, 1024), 1)
    y = (lane // 16) % 16
    z = lane % 16
    for s in range(slabs):
        cols = slice(s * 512, (s + 1) * 512)
        rim = slice(16 * s, 16 * s + 16)
        planes = jnp.concatenate([prev_ref[rim, :], parts[s][0:16, :], next_ref[rim, :]], axis=1).astype(F32)
        for b in (-1, 0, 1):
            for c in (-1, 0, 1):
                d = 16 * b + c
                moved = planes
                if d:
                    moved = pltpu.roll(planes, (-d) % 1024, 1)
                    ok = (y + b >= 0) & (y + b < 16) & (z + c >= 0) & (z + c < 16)
                    moved = jnp.where(ok, moved, 0.0)
                moved = moved.astype(BF16)
                for a in (-1, 0, 1):
                    tap = 9 * (a + 1) + 3 * (b + 1) + (c + 1)
                    at = (1 + a) * 256
                    x_ref[tap * 16 : (tap + 1) * 16, cols] = moved[:, at : at + 512]
        x_ref[ORDER:, cols] = parts[s][16:, :]
    for edge, start in zip(EDGES, STARTS):
        tile = nt(x_ref[edge:ORDER, :], x_ref[edge : edge + 128, :])
        out_ref[start : start + ORDER - edge, :] = tile
    out_ref[GRAD_AT : GRAD_AT + ORDER + 128, :] = nt(x_ref[...], x_ref[ORDER:, :])
    out_ref[COT_AT + 128 :, :] = jnp.zeros((PACKED - COT_AT - 128, 128), F32)
    for k in range(4):
        for half, ref in ((core, keep_ref), (1 - core, give_ref)):
            at = half * HALF + ((turn + k) % 4) * QUARTER
            ref[k * QUARTER : (k + 1) * QUARTER, :] = out_ref[pl.ds(pl.multiple_of(at, QUARTER), QUARTER), :]


def pair_kernel(keep_ref, got_ref, *outs):
    for k, out_ref in enumerate(outs):
        rows = slice(k * QUARTER, (k + 1) * QUARTER)
        out_ref[...] = keep_ref[rows, :] + got_ref[rows, :]


def fold_kernel(*refs):
    total = refs[0][...]
    for ref in refs[1:-1]:
        total = total + ref[...]
    refs[-1][...] = total


def fold_in_order_kernel(place_ref, *refs):
    parts, out_ref, slots = refs[:4], refs[4], refs[5]
    for k, ref in enumerate(parts):
        slots[(place_ref[4] + 4 - k) % 4] = ref[...]
    out_ref[...] = slots[0] + slots[1] + slots[2] + slots[3]


def scale_kernel(raw_ref, parts_ref, out_ref, *, size):
    total = parts_ref[0]
    for p in range(1, parts_ref.shape[0]):
        total = total + parts_ref[p]
    factor = jnp.sqrt(clip_rate * size / total)[0:1, :]
    out_ref[...] = raw_ref[...] * factor


def spread(row):
    return jnp.broadcast_to(row, (8, 128))


def sweep(tiles, g):
    shape = tiles[g].shape
    lane = lax.broadcasted_iota(jnp.int32, shape, 1)
    sub = lax.broadcasted_iota(jnp.int32, shape, 0)
    rows = tiles[g]

    def column(tile, q):
        return jnp.broadcast_to(tile[:, 8 * g + q : 8 * g + q + 1], shape)

    def row(tile, q):
        return jnp.broadcast_to(tile[q : q + 1, :], shape)

    cols = [column(rows, q) for q in range(8)]
    for k in range(0, 8, 2):
        one, two = cols[k], cols[k + 1]
        a, b, d = row(one, k), row(one, k + 1), row(two, k + 1)
        scale = 1.0 / (a * d - b * b)
        ia, ib, id_ = d * scale, -b * scale, a * scale
        upper, lower = sub == k, sub == k + 1
        for q in range(8):
            if q in (k, k + 1):
                continue
            h, l = row(cols[q], k), row(cols[q], k + 1)
            th, tl = ia * h + ib * l, ib * h + id_ * l
            rest = cols[q] - one * th - two * tl
            cols[q] = jnp.where(upper, th, jnp.where(lower, tl, rest))
        cols[k] = jnp.where(upper, ia, jnp.where(lower, ib, -(one * ia + two * ib)))
        cols[k + 1] = jnp.where(upper, ib, jnp.where(lower, id_, -(one * ib + two * id_)))
    terms = [cols[q] * row(rows, q) for q in range(8)]
    while len(terms) > 1:
        terms = [x + y for x, y in zip(terms[::2], terms[1::2])]
    swept = terms[0]
    for q in range(8):
        swept = jnp.where(lane == 8 * g + q, -cols[q], swept)
    heads = [row(swept, q) for q in range(8)]
    inside = (lane >= 8 * g) & (lane < 8 * g + 8)
    out = []
    for i, old in enumerate(tiles):
        if i == g:
            out.append(swept)
            continue
        new = jnp.where(inside, 0.0, old)
        for q in range(8):
            new = new - column(old, q) * heads[q]
        out.append(new)
    return out


def invert(mats, beside):
    held = [[m[8 * i : 8 * i + 8] for i in range(m.shape[0] // 8)] for m in mats]
    for g in range(len(held[0])):
        held = [sweep(tiles, g) for tiles in held]
        if beside:
            beside.pop(0)()
    while beside:
        beside.pop(0)()
    return [jnp.concatenate([-t for t in tiles], axis=0) for tiles in held]


STEP = 64
STEPS = tuple(range(0, ORDER, STEP))


def packed(col, row, rows):
    tile = col // 128
    at = STARTS[tile] + row - EDGES[tile]
    return slice(at, at + rows)


def forward_kernel(core_ref, *refs, count):
    mine, others = refs[:4], refs[4:8]
    z_ref, y_ref, right_ref, part_ref, stat_ref, b_ref = refs[8:]
    core, turn = core_ref[0], core_ref[1]
    for k in range(4):
        for half, ref in ((core, mine[k]), (1 - core, others[k])):
            at = half * HALF + ((turn + 4 - k) % 4) * QUARTER
            stat_ref[pl.ds(pl.multiple_of(at, QUARTER), QUARTER), :] = ref[...]
    eye = (
        lax.broadcasted_iota(jnp.int32, (128, 128), 0) == lax.broadcasted_iota(jnp.int32, (128, 128), 1)
    ).astype(F32)
    for p in range(4):
        edge = EDGES[p]
        head = min(128, ORDER - edge)
        rows = stat_ref[STARTS[p] : STARTS[p] + ORDER - edge, :] / count
        y_ref[STARTS[p] : STARTS[p] + ORDER - edge, :] = rows
        y_ref[STARTS[p] : STARTS[p] + head, :] = rows[:head] + damping * eye[:head]
    b_ref[...] = stat_ref[GRAD_AT : GRAD_AT + ORDER, :] / math.sqrt(count)
    right = stat_ref[COT_AT : COT_AT + 128, :] / count + damping * eye

    side = right[64:, :64]
    held = {}

    def first_half():
        held["y"] = nn(side, held["r"], HI)
        held["t"] = right[64:, 64:] - nt(held["y"], side, HI)

    def second_half():
        low = -nn(held["t"], held["y"], HI)
        top = held["r"] - tn(held["y"], low, HI)
        right_ref[0:64, 0:64] = top
        right_ref[0:64, 64:] = low.T
        right_ref[64:, 0:64] = low
        right_ref[64:, 64:] = held["t"]

    def first_rows():
        done = STEPS[-1]
        held["sum"] = tn(b_ref[0:done, :], z_ref[0:done, :], HI)

    beside = []
    d = y_ref[packed(0, 0, STEP), 0:STEP]
    for p, edge in enumerate(STEPS):
        size = min(STEP, ORDER - edge)
        half = (edge % 128) // STEP
        lanes = slice(half * STEP, half * STEP + size)
        below = edge + size
        left = ORDER - below
        if left == 0:
            beside.append(first_rows)
        if p == 0:
            w, held["r"] = invert([d, right[:64, :64]], beside)
            first_half()
        elif p == 1:
            w, held["t"] = invert([d, held["t"]], beside)
            beside.append(second_half)
        else:
            (w,) = invert([d], beside)
        if left == 0:
            z = nn(w, b_ref[edge:, :], HI)
            z_ref[edge:, :] = z
            held["sum"] = held["sum"] + tn(b_ref[edge:, :], z, HI)
            break
        low = y_ref[packed(edge, below, left), lanes]
        near = min(STEP, left)
        at = slice((1 - half) * STEP, (1 - half) * STEP + near)
        y_near = nn(low[:near], w, HI)
        d = y_ref[packed(below, below, near), at] - nt(y_near, low[:near], HI)

        def scale_rows(w=w, low=low, edge=edge, below=below, left=left, lanes=lanes):
            held["y_now"] = nn(low, w, HI)
            y_ref[packed(edge, below, left), lanes] = held["y_now"]

        def into_rhs(w=w, edge=edge, size=size, below=below):
            now = b_ref[edge : edge + size, :]
            z_ref[edge : edge + size, :] = nn(w, now, HI)
            b_ref[below:, :] = b_ref[below:, :] - nn(held["y_now"], now, HI)

        def into_half(low=low, edge=edge, below=below, left=left):
            span = packed(edge, below, left)
            y_ref[span, STEP:] = y_ref[span, STEP:] - nt(held["y_now"], low[:STEP], HI)

        def into_tile(tile, low=low, below=below):
            first = EDGES[tile] - below
            wide = min(128, ORDER - EDGES[tile])
            span = slice(STARTS[tile], STARTS[tile] + ORDER - EDGES[tile])
            y_ref[span, 0:wide] = y_ref[span, 0:wide] - nt(held["y_now"][first:], low[first : first + wide], HI)

        beside.append(scale_rows)
        if half == 0:
            beside.append(into_half)
        beside += [functools.partial(into_tile, tile) for tile in range(edge // 128 + 1, 4)]
        beside.append(into_rhs)
    prod = held["sum"] * right_ref[...]
    acc = prod[0:8]
    for i in range(1, 16):
        acc = acc + prod[8 * i : 8 * i + 8]
    part_ref[...] = jnp.broadcast_to(jnp.sum(acc).reshape(1, 1, 1), part_ref.shape)


def backward_kernel(z_ref, y_ref, right_ref, raw_ref, x_ref):
    for edge in reversed(STEPS):
        size = min(STEP, ORDER - edge)
        below = edge + size
        x = z_ref[edge : edge + size, :]
        if below < ORDER:
            lanes = slice(edge % 128, edge % 128 + size)
            y = y_ref[packed(edge, below, ORDER - below), lanes]
            x = x - tn(y, x_ref[below:, :], HI)
        x_ref[edge : edge + size, :] = x
    raw_ref[...] = nn(x_ref[...], right_ref[...], HI)


def on_device(activations, out_grad, kernel):
    shape = activations.shape
    spaces = lax.axis_size("space")
    groups = lax.axis_size("fac")
    wide = groups // 2
    act = activations.reshape(512, 128)
    cot = out_grad.reshape(512, 128)

    sp, fa = lax.axis_index("space"), lax.axis_index("fac")
    place = jnp.stack([sp % 2, sp // 2 % 4, fa // wide, fa % wide, sp // 8]).astype(jnp.int32)
    up = [(i, i + 1) for i in range(spaces - 1)]
    down = [(i + 1, i) for i in range(spaces - 1)]
    swap = [(i, i ^ 1) for i in range(spaces)]
    ends = [(i, (i + wide) % groups) for i in range(groups)]

    def ring_x(k):
        return [(i, i // wide * wide + (i + k) % wide) for i in range(groups)]

    def ring_y(k):
        return [(i, i // 8 * 8 + (i // 2 % 4 + k) % 4 * 2 + i % 2) for i in range(spaces)]

    def ring_z(k):
        return [(i, (i // 8 + k) % 4 * 8 + i % 8) for i in range(spaces)]

    def rows(count, width=128, dtype=F32):
        return jax.ShapeDtypeStruct((count, width), dtype)

    part = rows(144, 512, BF16)
    give, *sends = call(
        prep_kernel,
        (rows(192, 512, BF16),) + (part,) * 4,
        scratch=[pltpu.VMEM((128, 512), BF16)],
        name="prep",
    )(place, act, cot)
    got = lax.ppermute(give, "fac", ends)
    own = [sends[0]] + [lax.ppermute(sends[k], "fac", ring_x(k)) for k in (1, 2, 3)]
    got, own = lax.optimization_barrier((got, own))

    sends = call(spread_kernel, (part,) * 4, name="spread")(place, got)
    far = [sends[0]] + [lax.ppermute(sends[k], "fac", ring_x(k)) for k in (1, 2, 3)]
    parts = own + far

    first, last = call(rim_kernel, (rows(256, 256, BF16),) * 2, name="rim")(*parts)
    prev = lax.ppermute(last, "space", up)
    following = lax.ppermute(first, "space", down)

    keep, give = call(
        functools.partial(stats_kernel, slabs=groups),
        (rows(HALF),) * 2,
        scratch=[pltpu.VMEM((ORDER + 128, groups * 512), BF16), pltpu.VMEM((PACKED, 128), F32)],
        name="stats",
    )(place, prev, following, *parts)
    in_grad = call(
        in_grad_kernel,
        rows(512, 128, BF16),
        scratch=[pltpu.VMEM((1040, 128), F32), pltpu.VMEM((1152, 384), BF16)],
        name="in_grad",
    )(prev, cot, following, kernel)

    got = lax.ppermute(give, "space", swap)
    quarters = call(pair_kernel, (rows(QUARTER),) * 4, name="pair")(keep, got)
    over_y = [lax.ppermute(quarters[k], "space", ring_y(k)) for k in (1, 2, 3)]
    over_y, in_grad = lax.optimization_barrier((over_y, in_grad))
    mine = call(fold_kernel, rows(QUARTER), name="fold_y")(quarters[0], *over_y)
    over_z = [lax.ppermute(mine, "space", ring_z(k)) for k in (1, 2, 3)]
    mine = call(
        fold_in_order_kernel,
        rows(QUARTER),
        scratch=[pltpu.VMEM((4, QUARTER, 128), F32)],
        name="fold_z",
    )(place, mine, *over_z)
    mine = [mine] + [lax.ppermute(mine, "space", ring_y(k)) for k in (1, 2, 3)]
    others = [lax.ppermute(q, "space", swap) for q in mine]

    z, y, right, total = call(
        functools.partial(forward_kernel, count=float(512 * spaces * groups)),
        (rows(ORDER), rows(GRAD_AT), rows(128), jax.ShapeDtypeStruct((groups, 8, 128), F32)),
        scratch=[pltpu.VMEM((PACKED, 128), F32), pltpu.VMEM((ORDER, 128), F32)],
        name="forward",
    )(place, *mine, *others)
    every = lax.all_to_all(total, "fac", 0, 0, tiled=True)
    raw = call(backward_kernel, rows(ORDER), scratch=[pltpu.VMEM((ORDER, 128), F32)], name="backward")(z, y, right)
    update = call(functools.partial(scale_kernel, size=kernel.size), rows(ORDER), name="scale")(raw, every)
    return (in_grad.reshape(shape), update.reshape(TAPS, 16, 128))


def solution(mesh):
    placed = (P("fac", "space", None, None, None), P("fac", "space", None, None, None), P())
    return jax.shard_map(
        on_device,
        mesh=mesh,
        in_specs=placed,
        out_specs=(P("fac", "space", None, None, None), P(None, "fac", None)),
        check_vma=False,
    )
```

```python
import functools
import math

import jax
import jax.numpy as jnp
from jax import lax
from jax.experimental import pallas as pl
from jax.experimental.pallas import tpu as pltpu
from jax.sharding import PartitionSpec as P

damping = 0.1
clip_rate = 0.05
TAPS = 27
F32 = jnp.float32
BF16 = jnp.bfloat16
HI = lax.Precision.HIGHEST
VMEM = pl.BlockSpec(memory_space=pltpu.VMEM)
PARAMS = pltpu.CompilerParams(vmem_limit_bytes=48 * 1024 * 1024)

ORDER = 432
EDGES = (0, 128, 256, 384)
STARTS = (0, 432, 736, 912)
GRAD_AT = 960
COT_AT = 1392
PACKED = 1536
HALF = PACKED // 2
QUARTER = HALF // 4


def place():
    sp, fa = lax.axis_index("space"), lax.axis_index("fac")
    return sp % 2, sp // 2 % 4, fa // 4, fa % 4, sp // 8


def call(body, out_shape, scratch=(), name=None):
    def run(*args):
        return pl.pallas_call(
            body,
            out_shape=out_shape,
            in_specs=[VMEM] * len(args),
            out_specs=jax.tree.map(lambda _: VMEM, out_shape),
            scratch_shapes=list(scratch),
            compiler_params=PARAMS,
            name=name,
        )(*args)

    return run


def nt(a, b, precision=None):
    return lax.dot_general(a, b, (((1,), (1,)), ((), ())), precision=precision, preferred_element_type=F32)


def nn(a, b, precision=None):
    return lax.dot_general(a, b, (((1,), (0,)), ((), ())), precision=precision, preferred_element_type=F32)


def tn(a, b, precision=None):
    return lax.dot_general(a, b, (((0,), (0,)), ((), ())), precision=precision, preferred_element_type=F32)


def prep_kernel(act_ref, cot_ref, give_ref, *rest):
    sends, act_t = rest[:-1], rest[-1]
    half = act_ref.shape[1] // 2
    act_t[...] = act_ref[...].astype(F32).T.astype(BF16)
    cot = cot_ref[...].astype(F32).T.astype(BF16)
    _, _, high, turn, _ = place()
    give_ref[0:half, :] = act_t[pl.ds(pl.multiple_of((1 - high) * half, half), half), :]
    give_ref[half:, :] = cot
    for k, send_ref in enumerate(sends):
        at = high * half + ((turn + k) % 4) * 16
        send_ref[0:16, :] = act_t[pl.ds(pl.multiple_of(at, 16), 16), :]
        send_ref[16:, :] = cot


def spread_kernel(got_ref, *sends):
    half = got_ref.shape[0] - 128
    turn = place()[3]
    for k, send_ref in enumerate(sends):
        at = ((turn + k) % 4) * 16
        send_ref[0:16, :] = got_ref[pl.ds(pl.multiple_of(at, 16), 16), :]
        send_ref[16:, :] = got_ref[half:, :]


def rim_kernel(*refs):
    parts, (first_ref, last_ref) = refs[:-2], refs[-2:]
    for s, ref in enumerate(parts):
        first_ref[16 * s : 16 * s + 16, :] = ref[0:16, 0:256]
        last_ref[16 * s : 16 * s + 16, :] = ref[0:16, 256:]
    first_ref[128:, :] = parts[0][16:, 0:256]
    last_ref[128:, :] = parts[0][16:, 256:]


def in_grad_kernel(prev_ref, cot_ref, next_ref, kern_ref, out_ref, rows_ref, shift_ref):
    rows_ref[8:264, :] = prev_ref[128:, :].astype(F32).T
    rows_ref[264:776, :] = cot_ref[...].astype(F32)
    rows_ref[776:1032, :] = next_ref[128:, :].astype(F32).T
    z = lax.broadcasted_iota(jnp.int32, (256, 128), 0) % 16
    zeros = jnp.zeros((16, 384), BF16)
    for plane in range(4):
        base = plane * 288
        shift_ref[base : base + 16, :] = zeros
        shift_ref[base + 272 : base + 288, :] = zeros
        for n, c in enumerate((-1, 0, 1)):
            at = 8 + plane * 256 + c
            cells = rows_ref[at : at + 256, :]
            if c:
                cells = jnp.where((z + c >= 0) & (z + c < 16), cells, 0.0)
            shift_ref[base + 16 : base + 272, n * 128 : (n + 1) * 128] = cells.astype(BF16)
    for x in range(2):
        total = jnp.zeros((256, 128), F32)
        for a in (-1, 0, 1):
            for b in (-1, 0, 1):
                for n, c in enumerate((-1, 0, 1)):
                    tap = 9 * (1 - a) + 3 * (1 - b) + (1 - c)
                    at = (x + 1 + a) * 288 + 16 + 16 * b
                    rows = shift_ref[at : at + 256, n * 128 : (n + 1) * 128]
                    total = total + nt(rows, kern_ref[tap])
        out_ref[x * 256 : (x + 1) * 256, :] = total.astype(BF16)


def stats_kernel(prev_ref, next_ref, *refs, slabs):
    parts, (keep_ref, give_ref, x_ref, out_ref) = refs[:slabs], refs[slabs:]
    core, turn = place()[:2]
    lane = lax.broadcasted_iota(jnp.int32, (16, 1024), 1)
    y = (lane // 16) % 16
    z = lane % 16
    for s in range(slabs):
        cols = slice(s * 512, (s + 1) * 512)
        rim = slice(16 * s, 16 * s + 16)
        planes = jnp.concatenate([prev_ref[rim, :], parts[s][0:16, :], next_ref[rim, :]], axis=1).astype(F32)
        for b in (-1, 0, 1):
            for c in (-1, 0, 1):
                d = 16 * b + c
                moved = planes
                if d:
                    moved = pltpu.roll(planes, (-d) % 1024, 1)
                    ok = (y + b >= 0) & (y + b < 16) & (z + c >= 0) & (z + c < 16)
                    moved = jnp.where(ok, moved, 0.0)
                moved = moved.astype(BF16)
                for a in (-1, 0, 1):
                    tap = 9 * (a + 1) + 3 * (b + 1) + (c + 1)
                    at = (1 + a) * 256
                    x_ref[tap * 16 : (tap + 1) * 16, cols] = moved[:, at : at + 512]
        x_ref[ORDER:, cols] = parts[s][16:, :]
    for edge, start in zip(EDGES, STARTS):
        tile = nt(x_ref[edge:ORDER, :], x_ref[edge : edge + 128, :])
        out_ref[start : start + ORDER - edge, :] = tile
    out_ref[GRAD_AT : GRAD_AT + ORDER + 128, :] = nt(x_ref[...], x_ref[ORDER:, :])
    out_ref[COT_AT + 128 :, :] = jnp.zeros((PACKED - COT_AT - 128, 128), F32)
    for k in range(4):
        for half, ref in ((core, keep_ref), (1 - core, give_ref)):
            at = half * HALF + ((turn + k) % 4) * QUARTER
            ref[k * QUARTER : (k + 1) * QUARTER, :] = out_ref[pl.ds(pl.multiple_of(at, QUARTER), QUARTER), :]


def pair_kernel(keep_ref, got_ref, *outs):
    for k, out_ref in enumerate(outs):
        rows = slice(k * QUARTER, (k + 1) * QUARTER)
        out_ref[...] = keep_ref[rows, :] + got_ref[rows, :]


def fold_kernel(*refs):
    total = refs[0][...]
    for ref in refs[1:-1]:
        total = total + ref[...]
    refs[-1][...] = total


def fold_in_order_kernel(*refs):
    parts, out_ref, slots = refs[:4], refs[4], refs[5]
    z = place()[4]
    for k, ref in enumerate(parts):
        slots[(z + 4 - k) % 4] = ref[...]
    out_ref[...] = slots[0] + slots[1] + slots[2] + slots[3]


def scale_kernel(raw_ref, parts_ref, out_ref, *, size):
    total = parts_ref[0]
    for p in range(1, parts_ref.shape[0]):
        total = total + parts_ref[p]
    factor = jnp.sqrt(clip_rate * size / total)[0:1, :]
    out_ref[...] = raw_ref[...] * factor


def spread(row):
    return jnp.broadcast_to(row, (8, 128))


def sweep(tiles, g, cols):
    shape = tiles[g].shape
    lane = lax.broadcasted_iota(jnp.int32, shape, 1) - 8 * g
    sub = lax.broadcasted_iota(jnp.int32, shape, 0)
    rows = tiles[g]

    def column(tile, at):
        return jnp.broadcast_to(tile[:, at : at + 1], shape)

    def row(tile, q):
        return jnp.broadcast_to(tile[q : q + 1, :], shape)

    def add(terms):
        while len(terms) > 1:
            terms = [x + y for x, y in zip(terms[::2], terms[1::2])]
        return terms[0]

    cols = [column(rows, 8 * g + q) for q in range(8)] if cols is None else list(cols)
    more = g + 1 < len(tiles)
    if more:
        block = [column(tiles[g + 1], 8 * g + 8 + q) for q in range(8)]
        beside = [column(tiles[g + 1], 8 * g + q) for q in range(8)]
    for k in range(0, 8, 2):
        one, two = cols[k], cols[k + 1]
        a, b, d = row(one, k), row(one, k + 1), row(two, k + 1)
        scale = 1.0 / (a * d - b * b)
        ia, ib, id_ = d * scale, -b * scale, a * scale
        upper, lower = sub == k, sub == k + 1
        for q in range(8):
            if q in (k, k + 1):
                continue
            h, l = row(cols[q], k), row(cols[q], k + 1)
            th, tl = ia * h + ib * l, ib * h + id_ * l
            cols[q] = jnp.where(upper, th, jnp.where(lower, tl, cols[q] - (one * th + two * tl)))
        cols[k] = jnp.where(upper, ia, jnp.where(lower, ib, -(one * ia + two * ib)))
        cols[k + 1] = jnp.where(upper, ib, jnp.where(lower, id_, -(one * ib + two * id_)))
    ahead = None
    if more:
        ahead = []
        for q in range(8):
            t = add([cols[r] * row(beside[r], q) for r in range(8)])
            ahead.append(block[q] - add([beside[r] * row(t, r) for r in range(8)]))
    swept = add([cols[q] * row(rows, q) for q in range(8)])
    for q in range(8):
        swept = jnp.where(lane == q, -cols[q], swept)
    heads = [row(swept, q) for q in range(8)]
    inside = (lane >= 0) & (lane < 8)
    out = list(tiles)
    for i in range(g + 1, len(tiles)):
        old = tiles[i]
        heavy = beside if i == g + 1 else [column(old, 8 * g + q) for q in range(8)]
        out[i] = jnp.where(inside, 0.0, old) - add([c * h for c, h in zip(heavy, heads)])
    p = jnp.where(lane < 0, rows, jnp.where(lane == sub, -1.0, 0.0))
    s = jnp.where(lane < 8, swept, 0.0)
    return out, p, s, ahead


class Factor:
    def __init__(self, mat):
        self.tiles = [mat[8 * i : 8 * i + 8] for i in range(mat.shape[0] // 8)]
        self.left, self.right, self.cols = [], [], None

    def step(self):
        self.tiles, p, s, self.cols = sweep(self.tiles, len(self.left), self.cols)
        self.left.append(p)
        self.right.append(s)

    def parts(self):
        return jnp.concatenate(self.left, axis=0), jnp.concatenate(self.right, axis=0)


def factor(mat, beside):
    out = Factor(mat)
    for _ in out.tiles:
        out.step()
        if beside:
            beside.pop(0)()
    while beside:
        beside.pop(0)()
    return out.parts()


def packed(tile, row, rows):
    at = STARTS[tile] + row - EDGES[tile]
    return slice(at, at + rows)


def forward_kernel(*refs, count):
    mine, others = refs[:4], refs[4:8]
    z_ref, y_ref, right_ref, part_ref, stat_ref, b_ref = refs[8:]
    core, turn = place()[:2]
    for k in range(4):
        for half, ref in ((core, mine[k]), (1 - core, others[k])):
            at = half * HALF + ((turn + 4 - k) % 4) * QUARTER
            stat_ref[pl.ds(pl.multiple_of(at, QUARTER), QUARTER), :] = ref[...]
    eye = (
        lax.broadcasted_iota(jnp.int32, (128, 128), 0) == lax.broadcasted_iota(jnp.int32, (128, 128), 1)
    ).astype(F32)
    for t, edge in enumerate(EDGES):
        head = min(128, ORDER - edge)
        rows = stat_ref[packed(t, edge, ORDER - edge), :] / count
        y_ref[packed(t, edge, ORDER - edge), :] = rows
        y_ref[packed(t, edge, head), :] = rows[:head] + damping * eye[:head]
    b_ref[...] = stat_ref[GRAD_AT : GRAD_AT + ORDER, :] / math.sqrt(count)

    right = Factor(stat_ref[COT_AT : COT_AT + 128, :] / count + damping * eye)
    held = {}

    def idle():
        pass

    def finish_right():
        p, s = right.parts()
        right_ref[...] = tn(p, s, HI)

    beside = [right.step, idle] * 8
    d = y_ref[packed(0, 0, 128), :]
    for t, edge in enumerate(EDGES):
        size = min(128, ORDER - edge)
        below = edge + size
        left = ORDER - below
        if t == 1:
            work = beside
            beside = []
            for n in range(8):
                beside += work[n : n + 1] + [right.step]
            beside.append(finish_right)
        p, s = factor(d, beside)
        now = b_ref[edge:below, :]
        if left == 0:
            z = tn(p, nn(s, now, HI), HI)
            z_ref[edge:, :] = z
            held["sum"] = held["sum"] + tn(now, z, HI)
            break
        low = y_ref[packed(t, below, left), :]
        near = min(128, left)
        u_near, v_near = nt(low[:near], p, HI), nt(low[:near], s, HI)
        d = y_ref[packed(t + 1, below, near), 0:near] - nt(u_near, v_near, HI)

        def widen(low=low, p=p, s=s, u_near=u_near, v_near=v_near, near=near, left=left):
            held["u"], held["v"] = u_near, v_near
            if left > near:
                held["u"] = jnp.concatenate([u_near, nt(low[near:], p, HI)], axis=0)
                held["v"] = jnp.concatenate([v_near, nt(low[near:], s, HI)], axis=0)

        def into_tile(tile, low=low, below=below, near=near):
            first = max(EDGES[tile] - below, near)
            if first >= low.shape[0]:
                return
            at = EDGES[tile] - below
            wide = min(128, ORDER - EDGES[tile])
            span = packed(tile, below + first, low.shape[0] - first)
            y_ref[span, 0:wide] = y_ref[span, 0:wide] - nt(held["u"][first:], held["v"][at : at + wide], HI)

        def into_rhs(p=p, s=s, now=now, t=t, edge=edge, below=below, left=left):
            half = nn(s, now, HI)
            z = tn(p, half, HI)
            z_ref[edge:below, :] = z
            b_ref[below:, :] = b_ref[below:, :] - nn(held["u"], half, HI)
            term = tn(now, z, HI)
            held["sum"] = held["sum"] + term if t else term

        def scale_rows(s=s, t=t, below=below, left=left):
            y_ref[packed(t, below, left), :] = nn(held["u"], s, HI)

        beside = [widen] + [functools.partial(into_tile, r) for r in range(t + 1, len(EDGES))]
        beside += [into_rhs, scale_rows]
    prod = held["sum"] * right_ref[...]
    acc = prod[0:8]
    for i in range(1, 16):
        acc = acc + prod[8 * i : 8 * i + 8]
    part_ref[...] = jnp.broadcast_to(jnp.sum(acc).reshape(1, 1, 1), part_ref.shape)


def backward_kernel(z_ref, y_ref, right_ref, raw_ref, x_ref):
    for t in reversed(range(len(EDGES))):
        below = min(EDGES[t] + 128, ORDER)
        x = z_ref[EDGES[t] : below, :]
        if below < ORDER:
            x = x - tn(y_ref[packed(t, below, ORDER - below), :], x_ref[below:, :], HI)
        x_ref[EDGES[t] : below, :] = x
    raw_ref[...] = nn(x_ref[...], right_ref[...], HI)


def on_device(activations, out_grad, kernel):
    shape = activations.shape
    spaces = lax.axis_size("space")
    groups = lax.axis_size("fac")
    wide = groups // 2
    act = activations.reshape(512, 128)
    cot = out_grad.reshape(512, 128)

    up = [(i, i + 1) for i in range(spaces - 1)]
    down = [(i + 1, i) for i in range(spaces - 1)]
    swap = [(i, i ^ 1) for i in range(spaces)]
    ends = [(i, (i + wide) % groups) for i in range(groups)]

    def ring_x(k):
        return [(i, i // wide * wide + (i + k) % wide) for i in range(groups)]

    def ring_y(k):
        return [(i, i // 8 * 8 + (i // 2 % 4 + k) % 4 * 2 + i % 2) for i in range(spaces)]

    def ring_z(k):
        return [(i, (i // 8 + k) % 4 * 8 + i % 8) for i in range(spaces)]

    def rows(count, width=128, dtype=F32):
        return jax.ShapeDtypeStruct((count, width), dtype)

    part = rows(144, 512, BF16)
    give, *sends = call(
        prep_kernel,
        (rows(192, 512, BF16),) + (part,) * 4,
        scratch=[pltpu.VMEM((128, 512), BF16)],
        name="prep",
    )(act, cot)
    got = lax.ppermute(give, "fac", ends)
    own = [sends[0]] + [lax.ppermute(sends[k], "fac", ring_x(k)) for k in (1, 2, 3)]
    got, own = lax.optimization_barrier((got, own))

    sends = call(spread_kernel, (part,) * 4, name="spread")(got)
    far = [sends[0]] + [lax.ppermute(sends[k], "fac", ring_x(k)) for k in (1, 2, 3)]
    parts = own + far

    first, last = call(rim_kernel, (rows(256, 256, BF16),) * 2, name="rim")(*parts)
    prev = lax.ppermute(last, "space", up)
    following = lax.ppermute(first, "space", down)

    keep, give = call(
        functools.partial(stats_kernel, slabs=groups),
        (rows(HALF),) * 2,
        scratch=[pltpu.VMEM((ORDER + 128, groups * 512), BF16), pltpu.VMEM((PACKED, 128), F32)],
        name="stats",
    )(prev, following, *parts)
    in_grad = call(
        in_grad_kernel,
        rows(512, 128, BF16),
        scratch=[pltpu.VMEM((1040, 128), F32), pltpu.VMEM((1152, 384), BF16)],
        name="in_grad",
    )(prev, cot, following, kernel)

    got = lax.ppermute(give, "space", swap)
    quarters = call(pair_kernel, (rows(QUARTER),) * 4, name="pair")(keep, got)
    over_y = [lax.ppermute(quarters[k], "space", ring_y(k)) for k in (1, 2, 3)]
    over_y, in_grad = lax.optimization_barrier((over_y, in_grad))
    mine = call(fold_kernel, rows(QUARTER), name="fold_y")(quarters[0], *over_y)
    over_z = [lax.ppermute(mine, "space", ring_z(k)) for k in (1, 2, 3)]
    mine = call(
        fold_in_order_kernel,
        rows(QUARTER),
        scratch=[pltpu.VMEM((4, QUARTER, 128), F32)],
        name="fold_z",
    )(mine, *over_z)
    mine = [mine] + [lax.ppermute(mine, "space", ring_y(k)) for k in (1, 2, 3)]
    others = [lax.ppermute(q, "space", swap) for q in mine]

    z, y, right, total = call(
        functools.partial(forward_kernel, count=float(512 * spaces * groups)),
        (rows(ORDER), rows(GRAD_AT), rows(128), jax.ShapeDtypeStruct((groups, 8, 128), F32)),
        scratch=[pltpu.VMEM((PACKED, 128), F32), pltpu.VMEM((ORDER, 128), F32)],
        name="forward",
    )(*mine, *others)
    every = lax.all_to_all(total, "fac", 0, 0, tiled=True)
    raw = call(backward_kernel, rows(ORDER), scratch=[pltpu.VMEM((ORDER, 128), F32)], name="backward")(z, y, right)
    update = call(functools.partial(scale_kernel, size=kernel.size), rows(ORDER), name="scale")(raw, every)
    return (in_grad.reshape(shape), update.reshape(TAPS, 16, 128))


def solution(mesh):
    placed = (P("fac", "space", None, None, None), P("fac", "space", None, None, None), P())
    return jax.shard_map(
        on_device,
        mesh=mesh,
        in_specs=placed,
        out_specs=(P("fac", "space", None, None, None), P(None, "fac", None)),
        check_vma=False,
    )
```

```python
import functools
import math

import jax
import jax.numpy as jnp
from jax import lax
from jax.experimental import pallas as pl
from jax.experimental.pallas import tpu as pltpu
from jax.sharding import PartitionSpec as P

damping = 0.1
clip_rate = 0.05
TAPS = 27
F32 = jnp.float32
BF16 = jnp.bfloat16
HI = lax.Precision.HIGHEST
VMEM = pl.BlockSpec(memory_space=pltpu.VMEM)
PARAMS = pltpu.CompilerParams(vmem_limit_bytes=48 * 1024 * 1024)

ORDER = 432
EDGES = (0, 128, 256, 384)
STARTS = (0, 432, 736, 912)
GRAD_AT = 960
COT_AT = 1392
PACKED = 1536
HALF = PACKED // 2
QUARTER = HALF // 4


SMEM = pl.BlockSpec(memory_space=pltpu.SMEM)
ANY = pl.BlockSpec(memory_space=pl.ANY)


def call(body, out_shape, scratch=(), name=None, spec=VMEM):
    def run(*args):
        return pl.pallas_call(
            body,
            out_shape=out_shape,
            in_specs=[SMEM if a.dtype == jnp.int32 else spec for a in args],
            out_specs=jax.tree.map(lambda _: VMEM, out_shape),
            scratch_shapes=list(scratch),
            compiler_params=PARAMS,
            name=name,
        )(*args)

    return run


def nt(a, b, precision=None):
    return lax.dot_general(a, b, (((1,), (1,)), ((), ())), precision=precision, preferred_element_type=F32)


def nn(a, b, precision=None):
    return lax.dot_general(a, b, (((1,), (0,)), ((), ())), precision=precision, preferred_element_type=F32)


def tn(a, b, precision=None):
    return lax.dot_general(a, b, (((0,), (0,)), ((), ())), precision=precision, preferred_element_type=F32)


def prep_kernel(place_ref, act_any, cot_any, give_ref, *rest):
    sends, (act_ref, cot_ref, act_t, sems) = rest[:4], rest[4:]
    copies = [
        pltpu.make_async_copy(act_any, act_ref, sems.at[0]),
        pltpu.make_async_copy(cot_any, cot_ref, sems.at[1]),
    ]
    for copy in copies:
        copy.start()
    for copy in copies:
        copy.wait()
    half = act_ref.shape[1] // 2
    act_t[...] = act_ref[...].astype(F32).T.astype(BF16)
    cot = cot_ref[...].astype(F32).T.astype(BF16)
    high, turn = place_ref[2], place_ref[3]
    give_ref[half:, :] = cot
    for k, send_ref in enumerate(sends):
        block = ((turn + k) % 4) * 16
        give_ref[16 * k : 16 * k + 16, :] = act_t[pl.ds(pl.multiple_of((1 - high) * half + block, 16), 16), :]
        send_ref[0:16, :] = act_t[pl.ds(pl.multiple_of(high * half + block, 16), 16), :]
        send_ref[16:, :] = cot


def spread_kernel(got_ref, *sends):
    for k, send_ref in enumerate(sends):
        send_ref[0:16, :] = got_ref[16 * k : 16 * k + 16, :]
        send_ref[16:, :] = got_ref[16 * len(sends) :, :]


def rim_kernel(*refs):
    parts, (first_ref, last_ref) = refs[:-2], refs[-2:]
    for s, ref in enumerate(parts):
        first_ref[16 * s : 16 * s + 16, :] = ref[0:16, 0:256]
        last_ref[16 * s : 16 * s + 16, :] = ref[0:16, 256:]
    first_ref[128:, :] = parts[0][16:, 0:256]
    last_ref[128:, :] = parts[0][16:, 256:]


def in_grad_kernel(prev_ref, cot_ref, next_ref, kern_ref, out_ref, rows_ref, shift_ref):
    rows_ref[8:264, :] = prev_ref[128:, :].astype(F32).T
    rows_ref[264:776, :] = cot_ref[...].astype(F32)
    rows_ref[776:1032, :] = next_ref[128:, :].astype(F32).T
    z = lax.broadcasted_iota(jnp.int32, (256, 128), 0) % 16
    zeros = jnp.zeros((16, 384), BF16)
    for plane in range(4):
        base = plane * 288
        shift_ref[base : base + 16, :] = zeros
        shift_ref[base + 272 : base + 288, :] = zeros
        for n, c in enumerate((-1, 0, 1)):
            at = 8 + plane * 256 + c
            cells = rows_ref[at : at + 256, :]
            if c:
                cells = jnp.where((z + c >= 0) & (z + c < 16), cells, 0.0)
            shift_ref[base + 16 : base + 272, n * 128 : (n + 1) * 128] = cells.astype(BF16)
    for x in range(2):
        total = jnp.zeros((256, 128), F32)
        for a in (-1, 0, 1):
            for b in (-1, 0, 1):
                for n, c in enumerate((-1, 0, 1)):
                    tap = 9 * (1 - a) + 3 * (1 - b) + (1 - c)
                    at = (x + 1 + a) * 288 + 16 + 16 * b
                    rows = shift_ref[at : at + 256, n * 128 : (n + 1) * 128]
                    total = total + nt(rows, kern_ref[tap])
        out_ref[x * 256 : (x + 1) * 256, :] = total.astype(BF16)


def stats_kernel(place_ref, prev_ref, next_ref, *refs, slabs):
    parts, (keep_ref, give_ref, x_ref, out_ref) = refs[:slabs], refs[slabs:]
    core, turn = place_ref[0], place_ref[1]
    lane = lax.broadcasted_iota(jnp.int32, (16, 1024), 1)
    y = (lane // 16) % 16
    z = lane % 16
    for s in range(slabs):
        cols = slice(s * 512, (s + 1) * 512)
        rim = slice(16 * s, 16 * s + 16)
        planes = jnp.concatenate([prev_ref[rim, :], parts[s][0:16, :], next_ref[rim, :]], axis=1).astype(F32)
        for b in (-1, 0, 1):
            for c in (-1, 0, 1):
                d = 16 * b + c
                moved = planes
                if d:
                    moved = pltpu.roll(planes, (-d) % 1024, 1)
                    ok = (y + b >= 0) & (y + b < 16) & (z + c >= 0) & (z + c < 16)
                    moved = jnp.where(ok, moved, 0.0)
                moved = moved.astype(BF16)
                for a in (-1, 0, 1):
                    tap = 9 * (a + 1) + 3 * (b + 1) + (c + 1)
                    at = (1 + a) * 256
                    x_ref[tap * 16 : (tap + 1) * 16, cols] = moved[:, at : at + 512]
        x_ref[ORDER:, cols] = parts[s][16:, :]
    for edge, start in zip(EDGES, STARTS):
        tile = nt(x_ref[edge:ORDER, :], x_ref[edge : edge + 128, :])
        out_ref[start : start + ORDER - edge, :] = tile
    out_ref[GRAD_AT : GRAD_AT + ORDER + 128, :] = nt(x_ref[...], x_ref[ORDER:, :])
    out_ref[COT_AT + 128 :, :] = jnp.zeros((PACKED - COT_AT - 128, 128), F32)
    for k in range(4):
        for half, ref in ((core, keep_ref), (1 - core, give_ref)):
            at = half * HALF + ((turn + k) % 4) * QUARTER
            ref[k * QUARTER : (k + 1) * QUARTER, :] = out_ref[pl.ds(pl.multiple_of(at, QUARTER), QUARTER), :]


def pair_kernel(keep_ref, got_ref, *outs):
    for k, out_ref in enumerate(outs):
        rows = slice(k * QUARTER, (k + 1) * QUARTER)
        out_ref[...] = keep_ref[rows, :] + got_ref[rows, :]


def fold_kernel(*refs):
    total = refs[0][...]
    for ref in refs[1:-1]:
        total = total + ref[...]
    refs[-1][...] = total


def fold_ring_kernel(a_ref, b_ref, c_ref, d_ref, out_ref):
    out_ref[...] = (a_ref[...] + c_ref[...]) + (b_ref[...] + d_ref[...])


def scale_kernel(raw_ref, parts_ref, out_ref, *, size):
    total = parts_ref[0]
    for p in range(1, parts_ref.shape[0]):
        total = total + parts_ref[p]
    factor = jnp.sqrt(clip_rate * size / total)[0:1, :]
    out_ref[...] = raw_ref[...] * factor


def spread(row):
    return jnp.broadcast_to(row, (8, 128))


def sweep(tiles, g, cols):
    shape = tiles[g].shape
    lane = lax.broadcasted_iota(jnp.int32, shape, 1) - 8 * g
    sub = lax.broadcasted_iota(jnp.int32, shape, 0)
    rows = tiles[g]

    def column(tile, at):
        return jnp.broadcast_to(tile[:, at : at + 1], shape)

    def row(tile, q):
        return jnp.broadcast_to(tile[q : q + 1, :], shape)

    def add(terms):
        while len(terms) > 1:
            terms = [x + y for x, y in zip(terms[::2], terms[1::2])]
        return terms[0]

    cols = [column(rows, 8 * g + q) for q in range(8)] if cols is None else list(cols)
    more = g + 1 < len(tiles)
    if more:
        block = [column(tiles[g + 1], 8 * g + 8 + q) for q in range(8)]
        beside = [column(tiles[g + 1], 8 * g + q) for q in range(8)]
    for k in range(0, 8, 2):
        one, two = cols[k], cols[k + 1]
        a, b, d = row(one, k), row(one, k + 1), row(two, k + 1)
        scale = 1.0 / (a * d - b * b)
        ia, ib, id_ = d * scale, -b * scale, a * scale
        upper, lower = sub == k, sub == k + 1
        for q in range(8):
            if q in (k, k + 1):
                continue
            h, l = row(cols[q], k), row(cols[q], k + 1)
            th, tl = ia * h + ib * l, ib * h + id_ * l
            cols[q] = jnp.where(upper, th, jnp.where(lower, tl, cols[q] - (one * th + two * tl)))
        cols[k] = jnp.where(upper, ia, jnp.where(lower, ib, -(one * ia + two * ib)))
        cols[k + 1] = jnp.where(upper, ib, jnp.where(lower, id_, -(one * ib + two * id_)))
    ahead = None
    if more:
        ahead = []
        for q in range(8):
            t = add([cols[r] * row(beside[r], q) for r in range(8)])
            ahead.append(block[q] - add([beside[r] * row(t, r) for r in range(8)]))
    swept = add([cols[q] * row(rows, q) for q in range(8)])
    for q in range(8):
        swept = jnp.where(lane == q, -cols[q], swept)
    heads = [row(swept, q) for q in range(8)]
    inside = (lane >= 0) & (lane < 8)
    out = list(tiles)
    for i in range(g + 1, len(tiles)):
        old = tiles[i]
        heavy = beside if i == g + 1 else [column(old, 8 * g + q) for q in range(8)]
        out[i] = jnp.where(inside, 0.0, old) - add([c * h for c, h in zip(heavy, heads)])
    p = jnp.where(lane < 0, rows, jnp.where(lane == sub, -1.0, 0.0))
    s = jnp.where(lane < 8, swept, 0.0)
    return out, p, s, ahead


class Factor:
    def __init__(self, mat):
        self.tiles = [mat[8 * i : 8 * i + 8] for i in range(mat.shape[0] // 8)]
        self.left, self.right, self.cols = [], [], None

    def step(self):
        self.tiles, p, s, self.cols = sweep(self.tiles, len(self.left), self.cols)
        self.left.append(p)
        self.right.append(s)

    def parts(self):
        return jnp.concatenate(self.left, axis=0), jnp.concatenate(self.right, axis=0)


def factor(mat, beside):
    out = Factor(mat)
    for _ in out.tiles:
        out.step()
        if beside:
            beside.pop(0)()
    while beside:
        beside.pop(0)()
    return out.parts()


def packed(tile, row, rows):
    at = STARTS[tile] + row - EDGES[tile]
    return slice(at, at + rows)


def forward_kernel(place_ref, *refs, count):
    mine, others = refs[:4], refs[4:8]
    z_ref, y_ref, right_ref, part_ref, stat_ref, b_ref = refs[8:]
    core, turn = place_ref[0], place_ref[1]
    for k in range(4):
        for half, ref in ((core, mine[k]), (1 - core, others[k])):
            at = half * HALF + ((turn + 4 - k) % 4) * QUARTER
            stat_ref[pl.ds(pl.multiple_of(at, QUARTER), QUARTER), :] = ref[...]
    eye = (
        lax.broadcasted_iota(jnp.int32, (128, 128), 0) == lax.broadcasted_iota(jnp.int32, (128, 128), 1)
    ).astype(F32)
    for t, edge in enumerate(EDGES):
        head = min(128, ORDER - edge)
        rows = stat_ref[packed(t, edge, ORDER - edge), :] / count
        y_ref[packed(t, edge, ORDER - edge), :] = rows
        y_ref[packed(t, edge, head), :] = rows[:head] + damping * eye[:head]
    b_ref[...] = stat_ref[GRAD_AT : GRAD_AT + ORDER, :] / math.sqrt(count)

    right = Factor(stat_ref[COT_AT : COT_AT + 128, :] / count + damping * eye)
    held = {}

    def idle():
        pass

    def finish_right():
        p, s = right.parts()
        right_ref[...] = tn(p, s, HI)

    beside = [right.step, idle] * 8
    d = y_ref[packed(0, 0, 128), :]
    for t, edge in enumerate(EDGES):
        size = min(128, ORDER - edge)
        below = edge + size
        left = ORDER - below
        if t == 1:
            work = beside
            beside = []
            for n in range(8):
                beside += work[n : n + 1] + [right.step]
            beside.append(finish_right)
        p, s = factor(d, beside)
        now = b_ref[edge:below, :]
        if left == 0:
            z = tn(p, nn(s, now, HI), HI)
            z_ref[edge:, :] = z
            held["sum"] = held["sum"] + tn(now, z, HI)
            break
        low = y_ref[packed(t, below, left), :]
        near = min(128, left)
        u_near, v_near = nt(low[:near], p, HI), nt(low[:near], s, HI)
        d = y_ref[packed(t + 1, below, near), 0:near] - nt(u_near, v_near, HI)

        def widen(low=low, p=p, s=s, u_near=u_near, v_near=v_near, near=near, left=left):
            held["u"], held["v"] = u_near, v_near
            if left > near:
                held["u"] = jnp.concatenate([u_near, nt(low[near:], p, HI)], axis=0)
                held["v"] = jnp.concatenate([v_near, nt(low[near:], s, HI)], axis=0)

        def into_tile(tile, low=low, below=below, near=near):
            first = max(EDGES[tile] - below, near)
            if first >= low.shape[0]:
                return
            at = EDGES[tile] - below
            wide = min(128, ORDER - EDGES[tile])
            span = packed(tile, below + first, low.shape[0] - first)
            y_ref[span, 0:wide] = y_ref[span, 0:wide] - nt(held["u"][first:], held["v"][at : at + wide], HI)

        def into_rhs(p=p, s=s, now=now, t=t, edge=edge, below=below, left=left):
            half = nn(s, now, HI)
            z = tn(p, half, HI)
            z_ref[edge:below, :] = z
            b_ref[below:, :] = b_ref[below:, :] - nn(held["u"], half, HI)
            term = tn(now, z, HI)
            held["sum"] = held["sum"] + term if t else term

        def scale_rows(s=s, t=t, below=below, left=left):
            y_ref[packed(t, below, left), :] = nn(held["u"], s, HI)

        beside = [widen] + [functools.partial(into_tile, r) for r in range(t + 1, len(EDGES))]
        beside += [into_rhs, scale_rows]
    prod = held["sum"] * right_ref[...]
    acc = prod[0:8]
    for i in range(1, 16):
        acc = acc + prod[8 * i : 8 * i + 8]
    part_ref[...] = jnp.broadcast_to(jnp.sum(acc).reshape(1, 1, 1), part_ref.shape)


def backward_kernel(z_ref, y_ref, right_ref, raw_ref, x_ref):
    for t in reversed(range(len(EDGES))):
        below = min(EDGES[t] + 128, ORDER)
        x = z_ref[EDGES[t] : below, :]
        if below < ORDER:
            x = x - tn(y_ref[packed(t, below, ORDER - below), :], x_ref[below:, :], HI)
        x_ref[EDGES[t] : below, :] = x
    raw_ref[...] = nn(x_ref[...], right_ref[...], HI)


def on_device(activations, out_grad, kernel):
    shape = activations.shape
    spaces = lax.axis_size("space")
    groups = lax.axis_size("fac")
    wide = groups // 2
    act = activations.reshape(512, 128)
    cot = out_grad.reshape(512, 128)

    sp, fa = lax.axis_index("space"), lax.axis_index("fac")
    place = jnp.stack([sp % 2, sp // 2 % 4, fa // wide, fa % wide]).astype(jnp.int32)
    up = [(i, i + 1) for i in range(spaces - 1)]
    down = [(i + 1, i) for i in range(spaces - 1)]
    swap = [(i, i ^ 1) for i in range(spaces)]
    ends = [(i, (i + wide) % groups) for i in range(groups)]

    def ring_x(k):
        return [(i, i // wide * wide + (i + k) % wide) for i in range(groups)]

    def ring_y(k):
        return [(i, i // 8 * 8 + (i // 2 % 4 + k) % 4 * 2 + i % 2) for i in range(spaces)]

    def ring_z(k):
        return [(i, (i // 8 + k) % 4 * 8 + i % 8) for i in range(spaces)]

    def rows(count, width=128, dtype=F32):
        return jax.ShapeDtypeStruct((count, width), dtype)

    part = rows(144, 512, BF16)
    give, *sends = call(
        prep_kernel,
        (rows(192, 512, BF16),) + (part,) * 4,
        scratch=[pltpu.VMEM((512, 128), BF16)] * 2 + [pltpu.VMEM((128, 512), BF16), pltpu.SemaphoreType.DMA((2,))],
        name="prep",
        spec=ANY,
    )(place, act, cot)
    got = lax.ppermute(give, "fac", ends)
    own = [sends[0]] + [lax.ppermute(sends[k], "fac", ring_x(k)) for k in (1, 2, 3)]
    got, own = lax.optimization_barrier((got, own))

    sends = call(spread_kernel, (part,) * 4, name="spread")(got)
    far = [sends[0]] + [lax.ppermute(sends[k], "fac", ring_x(k)) for k in (1, 2, 3)]
    parts = own + far

    first, last = call(rim_kernel, (rows(256, 256, BF16),) * 2, name="rim")(*parts)
    prev = lax.ppermute(last, "space", up)
    following = lax.ppermute(first, "space", down)

    keep, give = call(
        functools.partial(stats_kernel, slabs=groups),
        (rows(HALF),) * 2,
        scratch=[pltpu.VMEM((ORDER + 128, groups * 512), BF16), pltpu.VMEM((PACKED, 128), F32)],
        name="stats",
    )(place, prev, following, *parts)
    in_grad = call(
        in_grad_kernel,
        rows(512, 128, BF16),
        scratch=[pltpu.VMEM((1040, 128), F32), pltpu.VMEM((1152, 384), BF16)],
        name="in_grad",
    )(prev, cot, following, kernel)

    got = lax.ppermute(give, "space", swap)
    quarters = call(pair_kernel, (rows(QUARTER),) * 4, name="pair")(keep, got)
    over_y = [lax.ppermute(quarters[k], "space", ring_y(k)) for k in (1, 2, 3)]
    over_y, in_grad = lax.optimization_barrier((over_y, in_grad))
    mine = call(fold_kernel, rows(QUARTER), name="fold_y")(quarters[0], *over_y)
    over_z = [lax.ppermute(mine, "space", ring_z(k)) for k in (1, 2, 3)]
    mine = call(fold_ring_kernel, rows(QUARTER), name="fold_z")(mine, *over_z)
    mine = [mine] + [lax.ppermute(mine, "space", ring_y(k)) for k in (1, 2, 3)]
    others = [lax.ppermute(q, "space", swap) for q in mine]

    z, y, right, total = call(
        functools.partial(forward_kernel, count=float(512 * spaces * groups)),
        (rows(ORDER), rows(GRAD_AT), rows(128), jax.ShapeDtypeStruct((groups, 8, 128), F32)),
        scratch=[pltpu.VMEM((PACKED, 128), F32), pltpu.VMEM((ORDER, 128), F32)],
        name="forward",
    )(place, *mine, *others)
    every = lax.all_to_all(total, "fac", 0, 0, tiled=True)
    raw = call(backward_kernel, rows(ORDER), scratch=[pltpu.VMEM((ORDER, 128), F32)], name="backward")(z, y, right)
    update = call(functools.partial(scale_kernel, size=kernel.size), rows(ORDER), name="scale")(raw, every)
    return (in_grad.reshape(shape), update.reshape(TAPS, 16, 128))


def solution(mesh):
    placed = (P("fac", "space", None, None, None), P("fac", "space", None, None, None), P())
    return jax.shard_map(
        on_device,
        mesh=mesh,
        in_specs=placed,
        out_specs=(P("fac", "space", None, None, None), P(None, "fac", None)),
        check_vma=False,
    )
```

```python
import functools
import math

import jax
import jax.numpy as jnp
from jax import lax
from jax.experimental import pallas as pl
from jax.experimental.pallas import tpu as pltpu
from jax.sharding import PartitionSpec as P

damping = 0.1
clip_rate = 0.05
TAPS = 27
F32 = jnp.float32
BF16 = jnp.bfloat16
HI = lax.Precision.HIGHEST
VMEM = pl.BlockSpec(memory_space=pltpu.VMEM)

ORDER = 432
EDGES = (0, 128, 256, 384)
STARTS = (0, 432, 736, 912)
GRAD_AT = 960
COT_AT = 1392
PACKED = 1536
HALF = PACKED // 2
QUARTER = HALF // 4


SMEM = pl.BlockSpec(memory_space=pltpu.SMEM)
ANY = pl.BlockSpec(memory_space=pl.ANY)


def call(body, out_shape, scratch=(), name=None, spec=VMEM, grant=48):
    def run(*args):
        return pl.pallas_call(
            body,
            out_shape=out_shape,
            in_specs=[SMEM if a.dtype == jnp.int32 else spec for a in args],
            out_specs=jax.tree.map(lambda _: VMEM, out_shape),
            scratch_shapes=list(scratch),
            compiler_params=pltpu.CompilerParams(vmem_limit_bytes=grant * 1024 * 1024),
            name=name,
        )(*args)

    return run


def nt(a, b, precision=None):
    return lax.dot_general(a, b, (((1,), (1,)), ((), ())), precision=precision, preferred_element_type=F32)


def nn(a, b, precision=None):
    return lax.dot_general(a, b, (((1,), (0,)), ((), ())), precision=precision, preferred_element_type=F32)


def tn(a, b, precision=None):
    return lax.dot_general(a, b, (((0,), (0,)), ((), ())), precision=precision, preferred_element_type=F32)


def prep_kernel(place_ref, act_any, cot_any, give_ref, *rest):
    sends, (act_ref, cot_ref, act_t, sems) = rest[:4], rest[4:]
    copies = [
        pltpu.make_async_copy(act_any, act_ref, sems.at[0]),
        pltpu.make_async_copy(cot_any, cot_ref, sems.at[1]),
    ]
    for copy in copies:
        copy.start()
    for copy in copies:
        copy.wait()
    half = act_ref.shape[1] // 2
    act_t[...] = act_ref[...].astype(F32).T.astype(BF16)
    cot = cot_ref[...].astype(F32).T.astype(BF16)
    high, turn = place_ref[2], place_ref[3]
    give_ref[half:, :] = cot
    for k, send_ref in enumerate(sends):
        block = ((turn + k) % 4) * 16
        give_ref[16 * k : 16 * k + 16, :] = act_t[pl.ds(pl.multiple_of((1 - high) * half + block, 16), 16), :]
        send_ref[0:16, :] = act_t[pl.ds(pl.multiple_of(high * half + block, 16), 16), :]
        send_ref[16:, :] = cot


def spread_kernel(got_ref, *sends):
    for k, send_ref in enumerate(sends):
        send_ref[0:16, :] = got_ref[16 * k : 16 * k + 16, :]
        send_ref[16:, :] = got_ref[16 * len(sends) :, :]


def rim_kernel(*refs):
    parts, (first_ref, last_ref) = refs[:-2], refs[-2:]
    for s, ref in enumerate(parts):
        first_ref[16 * s : 16 * s + 16, :] = ref[0:16, 0:256]
        last_ref[16 * s : 16 * s + 16, :] = ref[0:16, 256:]
    first_ref[128:, :] = parts[0][16:, 0:256]
    last_ref[128:, :] = parts[0][16:, 256:]


def in_grad_kernel(prev_ref, cot_ref, next_ref, kern_ref, out_ref, rows_ref, shift_ref):
    rows_ref[8:264, :] = prev_ref[128:, :].astype(F32).T
    rows_ref[264:776, :] = cot_ref[...].astype(F32)
    rows_ref[776:1032, :] = next_ref[128:, :].astype(F32).T
    z = lax.broadcasted_iota(jnp.int32, (256, 128), 0) % 16
    zeros = jnp.zeros((16, 384), BF16)
    for plane in range(4):
        base = plane * 288
        shift_ref[base : base + 16, :] = zeros
        shift_ref[base + 272 : base + 288, :] = zeros
        for n, c in enumerate((-1, 0, 1)):
            at = 8 + plane * 256 + c
            cells = rows_ref[at : at + 256, :]
            if c:
                cells = jnp.where((z + c >= 0) & (z + c < 16), cells, 0.0)
            shift_ref[base + 16 : base + 272, n * 128 : (n + 1) * 128] = cells.astype(BF16)
    for x in range(2):
        total = jnp.zeros((256, 128), F32)
        for a in (-1, 0, 1):
            for b in (-1, 0, 1):
                for n, c in enumerate((-1, 0, 1)):
                    tap = 9 * (1 - a) + 3 * (1 - b) + (1 - c)
                    at = (x + 1 + a) * 288 + 16 + 16 * b
                    rows = shift_ref[at : at + 256, n * 128 : (n + 1) * 128]
                    total = total + nt(rows, kern_ref[tap])
        out_ref[x * 256 : (x + 1) * 256, :] = total.astype(BF16)


def stats_kernel(place_ref, prev_ref, next_ref, *refs, slabs):
    parts, (keep_ref, give_ref, x_ref, out_ref) = refs[:slabs], refs[slabs:]
    core, turn = place_ref[0], place_ref[1]
    lane = lax.broadcasted_iota(jnp.int32, (16, 1024), 1)
    y = (lane // 16) % 16
    z = lane % 16
    for s in range(slabs):
        cols = slice(s * 512, (s + 1) * 512)
        rim = slice(16 * s, 16 * s + 16)
        planes = jnp.concatenate([prev_ref[rim, :], parts[s][0:16, :], next_ref[rim, :]], axis=1).astype(F32)
        for b in (-1, 0, 1):
            for c in (-1, 0, 1):
                d = 16 * b + c
                moved = planes
                if d:
                    moved = pltpu.roll(planes, (-d) % 1024, 1)
                    ok = (y + b >= 0) & (y + b < 16) & (z + c >= 0) & (z + c < 16)
                    moved = jnp.where(ok, moved, 0.0)
                moved = moved.astype(BF16)
                for a in (-1, 0, 1):
                    tap = 9 * (a + 1) + 3 * (b + 1) + (c + 1)
                    at = (1 + a) * 256
                    x_ref[128 + tap * 16 : 144 + tap * 16, cols] = moved[:, at : at + 512]
        x_ref[0:128, cols] = parts[s][16:, :]
    wide = nt(x_ref[...], x_ref[0:256, :])
    out_ref[COT_AT : COT_AT + 128, :] = wide[:128, :128]
    out_ref[GRAD_AT : GRAD_AT + ORDER, :] = wide[128:, :128]
    out_ref[STARTS[0] : STARTS[0] + ORDER, :] = wide[128:, 128:]
    wide = nt(x_ref[256:, :], x_ref[256:512, :])
    out_ref[STARTS[1] : STARTS[1] + ORDER - 128, :] = wide[:, :128]
    out_ref[STARTS[2] : STARTS[2] + ORDER - 256, :] = wide[128:, 128:]
    out_ref[STARTS[3] : STARTS[3] + ORDER - 384, :] = jnp.zeros((ORDER - 384, 128), F32)
    out_ref[STARTS[3] : STARTS[3] + ORDER - 384, 0 : ORDER - 384] = nt(x_ref[512:, :], x_ref[512:, :])
    out_ref[COT_AT + 128 :, :] = jnp.zeros((PACKED - COT_AT - 128, 128), F32)
    for k in range(4):
        for half, ref in ((core, keep_ref), (1 - core, give_ref)):
            at = half * HALF + ((turn + k) % 4) * QUARTER
            ref[k * QUARTER : (k + 1) * QUARTER, :] = out_ref[pl.ds(pl.multiple_of(at, QUARTER), QUARTER), :]


def pair_kernel(keep_ref, got_ref, *outs):
    for k, out_ref in enumerate(outs):
        rows = slice(k * QUARTER, (k + 1) * QUARTER)
        out_ref[...] = keep_ref[rows, :] + got_ref[rows, :]


def fold_kernel(*refs):
    total = refs[0][...]
    for ref in refs[1:-1]:
        total = total + ref[...]
    refs[-1][...] = total


def fold_ring_kernel(a_ref, b_ref, c_ref, d_ref, out_ref):
    out_ref[...] = (a_ref[...] + c_ref[...]) + (b_ref[...] + d_ref[...])


def scale_kernel(raw_ref, parts_ref, out_ref, *, size):
    total = parts_ref[0]
    for p in range(1, parts_ref.shape[0]):
        total = total + parts_ref[p]
    factor = jnp.sqrt(clip_rate * size / total)[0:1, :]
    out_ref[...] = raw_ref[...] * factor


def spread(row):
    return jnp.broadcast_to(row, (8, 128))


def sweep(tiles, g, cols):
    shape = tiles[g].shape
    lane = lax.broadcasted_iota(jnp.int32, shape, 1) - 8 * g
    sub = lax.broadcasted_iota(jnp.int32, shape, 0)
    rows = tiles[g]

    def column(tile, at):
        return jnp.broadcast_to(tile[:, at : at + 1], shape)

    def row(tile, q):
        return jnp.broadcast_to(tile[q : q + 1, :], shape)

    def add(terms):
        while len(terms) > 1:
            terms = [x + y for x, y in zip(terms[::2], terms[1::2])]
        return terms[0]

    cols = [column(rows, 8 * g + q) for q in range(8)] if cols is None else list(cols)
    more = g + 1 < len(tiles)
    if more:
        block = [column(tiles[g + 1], 8 * g + 8 + q) for q in range(8)]
        beside = [column(tiles[g + 1], 8 * g + q) for q in range(8)]
    for k in range(0, 8, 2):
        one, two = cols[k], cols[k + 1]
        a, b, d = row(one, k), row(one, k + 1), row(two, k + 1)
        scale = 1.0 / (a * d - b * b)
        ia, ib, id_ = d * scale, -b * scale, a * scale
        upper, lower = sub == k, sub == k + 1
        for q in range(8):
            if q in (k, k + 1):
                continue
            h, l = row(cols[q], k), row(cols[q], k + 1)
            th, tl = ia * h + ib * l, ib * h + id_ * l
            cols[q] = jnp.where(upper, th, jnp.where(lower, tl, cols[q] - (one * th + two * tl)))
        cols[k] = jnp.where(upper, ia, jnp.where(lower, ib, -(one * ia + two * ib)))
        cols[k + 1] = jnp.where(upper, ib, jnp.where(lower, id_, -(one * ib + two * id_)))
    ahead = None
    if more:
        ahead = []
        for q in range(8):
            t = add([cols[r] * row(beside[r], q) for r in range(8)])
            ahead.append(block[q] - add([beside[r] * row(t, r) for r in range(8)]))
    swept = add([cols[q] * row(rows, q) for q in range(8)])
    for q in range(8):
        swept = jnp.where(lane == q, -cols[q], swept)
    heads = [row(swept, q) for q in range(8)]
    inside = (lane >= 0) & (lane < 8)
    out = list(tiles)
    for i in range(g + 1, len(tiles)):
        old = tiles[i]
        heavy = beside if i == g + 1 else [column(old, 8 * g + q) for q in range(8)]
        out[i] = jnp.where(inside, 0.0, old) - add([c * h for c, h in zip(heavy, heads)])
    p = jnp.where(lane < 0, rows, jnp.where(lane == sub, -1.0, 0.0))
    s = jnp.where(lane < 8, swept, 0.0)
    return out, p, s, ahead


class Factor:
    def __init__(self, mat):
        self.tiles = [mat[8 * i : 8 * i + 8] for i in range(mat.shape[0] // 8)]
        self.left, self.right, self.cols = [], [], None

    def step(self):
        self.tiles, p, s, self.cols = sweep(self.tiles, len(self.left), self.cols)
        self.left.append(p)
        self.right.append(s)

    def parts(self):
        return jnp.concatenate(self.left, axis=0), jnp.concatenate(self.right, axis=0)


def factor(mat, beside):
    out = Factor(mat)
    for _ in out.tiles:
        out.step()
        if beside:
            beside.pop(0)()
    while beside:
        beside.pop(0)()
    return out.parts()


def packed(tile, row, rows):
    at = STARTS[tile] + row - EDGES[tile]
    return slice(at, at + rows)


def forward_kernel(place_ref, *refs, count):
    mine, others = refs[:4], refs[4:8]
    z_ref, y_ref, right_ref, part_ref, stat_ref, b_ref = refs[8:]
    core, turn = place_ref[0], place_ref[1]
    for k in range(4):
        for half, ref in ((core, mine[k]), (1 - core, others[k])):
            at = half * HALF + ((turn + 4 - k) % 4) * QUARTER
            stat_ref[pl.ds(pl.multiple_of(at, QUARTER), QUARTER), :] = ref[...]
    eye = (
        lax.broadcasted_iota(jnp.int32, (128, 128), 0) == lax.broadcasted_iota(jnp.int32, (128, 128), 1)
    ).astype(F32)
    for t, edge in enumerate(EDGES):
        head = min(128, ORDER - edge)
        rows = stat_ref[packed(t, edge, ORDER - edge), :] / count
        y_ref[packed(t, edge, ORDER - edge), :] = rows
        y_ref[packed(t, edge, head), :] = rows[:head] + damping * eye[:head]
    b_ref[...] = stat_ref[GRAD_AT : GRAD_AT + ORDER, :] / math.sqrt(count)

    right = Factor(stat_ref[COT_AT : COT_AT + 128, :] / count + damping * eye)
    held = {}

    def idle():
        pass

    def finish_right():
        p, s = right.parts()
        right_ref[...] = tn(p, s, HI)

    beside = [right.step, idle] * 8
    d = y_ref[packed(0, 0, 128), :]
    for t, edge in enumerate(EDGES):
        size = min(128, ORDER - edge)
        below = edge + size
        left = ORDER - below
        if t == 1:
            work = beside
            beside = []
            for n in range(8):
                beside += work[n : n + 1] + [right.step]
            beside.append(finish_right)
        p, s = factor(d, beside)
        now = b_ref[edge:below, :]
        if left == 0:
            z = tn(p, nn(s, now, HI), HI)
            z_ref[edge:, :] = z
            held["sum"] = held["sum"] + tn(now, z, HI)
            break
        low = y_ref[packed(t, below, left), :]
        near = min(128, left)
        u_near, v_near = nt(low[:near], p, HI), nt(low[:near], s, HI)
        d = y_ref[packed(t + 1, below, near), 0:near] - nt(u_near, v_near, HI)

        def widen(low=low, p=p, s=s, u_near=u_near, v_near=v_near, near=near, left=left):
            held["u"], held["v"] = u_near, v_near
            if left > near:
                held["u"] = jnp.concatenate([u_near, nt(low[near:], p, HI)], axis=0)
                held["v"] = jnp.concatenate([v_near, nt(low[near:], s, HI)], axis=0)

        def into_tile(tile, low=low, below=below, near=near):
            first = max(EDGES[tile] - below, near)
            if first >= low.shape[0]:
                return
            at = EDGES[tile] - below
            wide = min(128, ORDER - EDGES[tile])
            span = packed(tile, below + first, low.shape[0] - first)
            y_ref[span, 0:wide] = y_ref[span, 0:wide] - nt(held["u"][first:], held["v"][at : at + wide], HI)

        def into_rhs(p=p, s=s, now=now, t=t, edge=edge, below=below, left=left):
            half = nn(s, now, HI)
            z = tn(p, half, HI)
            z_ref[edge:below, :] = z
            b_ref[below:, :] = b_ref[below:, :] - nn(held["u"], half, HI)
            term = tn(now, z, HI)
            held["sum"] = held["sum"] + term if t else term

        def scale_rows(s=s, t=t, below=below, left=left):
            y_ref[packed(t, below, left), :] = nn(held["u"], s, HI)

        beside = [widen] + [functools.partial(into_tile, r) for r in range(t + 1, len(EDGES))]
        beside += [into_rhs, scale_rows]
    prod = held["sum"] * right_ref[...]
    acc = prod[0:8]
    for i in range(1, 16):
        acc = acc + prod[8 * i : 8 * i + 8]
    part_ref[...] = jnp.broadcast_to(jnp.sum(acc).reshape(1, 1, 1), part_ref.shape)


def backward_kernel(z_ref, y_ref, right_ref, raw_ref, x_ref):
    for t in reversed(range(len(EDGES))):
        below = min(EDGES[t] + 128, ORDER)
        x = z_ref[EDGES[t] : below, :]
        if below < ORDER:
            x = x - tn(y_ref[packed(t, below, ORDER - below), :], x_ref[below:, :], HI)
        x_ref[EDGES[t] : below, :] = x
    raw_ref[...] = nn(x_ref[...], right_ref[...], HI)


def on_device(activations, out_grad, kernel):
    shape = activations.shape
    spaces = lax.axis_size("space")
    groups = lax.axis_size("fac")
    wide = groups // 2
    act = activations.reshape(512, 128)
    cot = out_grad.reshape(512, 128)

    sp, fa = lax.axis_index("space"), lax.axis_index("fac")
    place = jnp.stack([sp % 2, sp // 2 % 4, fa // wide, fa % wide]).astype(jnp.int32)
    up = [(i, i + 1) for i in range(spaces - 1)]
    down = [(i + 1, i) for i in range(spaces - 1)]
    swap = [(i, i ^ 1) for i in range(spaces)]
    ends = [(i, (i + wide) % groups) for i in range(groups)]

    def ring_x(k):
        return [(i, i // wide * wide + (i + k) % wide) for i in range(groups)]

    def ring_y(k):
        return [(i, i // 8 * 8 + (i // 2 % 4 + k) % 4 * 2 + i % 2) for i in range(spaces)]

    def ring_z(k):
        return [(i, (i // 8 + k) % 4 * 8 + i % 8) for i in range(spaces)]

    def rows(count, width=128, dtype=F32):
        return jax.ShapeDtypeStruct((count, width), dtype)

    part = rows(144, 512, BF16)
    give, *sends = call(
        prep_kernel,
        (rows(192, 512, BF16),) + (part,) * 4,
        scratch=[pltpu.VMEM((512, 128), BF16)] * 2 + [pltpu.VMEM((128, 512), BF16), pltpu.SemaphoreType.DMA((2,))],
        name="prep",
        spec=ANY,
        grant=60,
    )(place, act, cot)
    got = lax.ppermute(give, "fac", ends)
    own = [sends[0]] + [lax.ppermute(sends[k], "fac", ring_x(k)) for k in (1, 2, 3)]
    got, own = lax.optimization_barrier((got, own))

    sends = call(spread_kernel, (part,) * 4, name="spread")(got)
    far = [sends[0]] + [lax.ppermute(sends[k], "fac", ring_x(k)) for k in (1, 2, 3)]
    parts = own + far

    first, last = call(rim_kernel, (rows(256, 256, BF16),) * 2, name="rim")(*parts)
    prev = lax.ppermute(last, "space", up)
    following = lax.ppermute(first, "space", down)

    keep, give = call(
        functools.partial(stats_kernel, slabs=groups),
        (rows(HALF),) * 2,
        scratch=[pltpu.VMEM((ORDER + 128, groups * 512), BF16), pltpu.VMEM((PACKED, 128), F32)],
        name="stats",
    )(place, prev, following, *parts)
    in_grad = call(
        in_grad_kernel,
        rows(512, 128, BF16),
        scratch=[pltpu.VMEM((1040, 128), F32), pltpu.VMEM((1152, 384), BF16)],
        name="in_grad",
    )(prev, cot, following, kernel)

    got = lax.ppermute(give, "space", swap)
    quarters = call(pair_kernel, (rows(QUARTER),) * 4, name="pair")(keep, got)
    over_y = [lax.ppermute(quarters[k], "space", ring_y(k)) for k in (1, 2, 3)]
    over_y, in_grad = lax.optimization_barrier((over_y, in_grad))
    mine = call(fold_kernel, rows(QUARTER), name="fold_y")(quarters[0], *over_y)
    over_z = [lax.ppermute(mine, "space", ring_z(k)) for k in (1, 2, 3)]
    mine = call(fold_ring_kernel, rows(QUARTER), name="fold_z")(mine, *over_z)
    mine = [mine] + [lax.ppermute(mine, "space", ring_y(k)) for k in (1, 2, 3)]
    others = [lax.ppermute(q, "space", swap) for q in mine]

    z, y, right, total = call(
        functools.partial(forward_kernel, count=float(512 * spaces * groups)),
        (rows(ORDER), rows(GRAD_AT), rows(128), jax.ShapeDtypeStruct((groups, 8, 128), F32)),
        scratch=[pltpu.VMEM((PACKED, 128), F32), pltpu.VMEM((ORDER, 128), F32)],
        name="forward",
    )(place, *mine, *others)
    every = lax.all_to_all(total, "fac", 0, 0, tiled=True)
    raw = call(backward_kernel, rows(ORDER), scratch=[pltpu.VMEM((ORDER, 128), F32)], name="backward")(z, y, right)
    update = call(functools.partial(scale_kernel, size=kernel.size), rows(ORDER), name="scale")(raw, every)
    return (in_grad.reshape(shape), update.reshape(TAPS, 16, 128))


def solution(mesh):
    placed = (P("fac", "space", None, None, None), P("fac", "space", None, None, None), P())
    return jax.shard_map(
        on_device,
        mesh=mesh,
        in_specs=placed,
        out_specs=(P("fac", "space", None, None, None), P(None, "fac", None)),
        check_vma=False,
    )
```
